128 devices in a mesh: freq: 8 (over x, core), bl: 16 (over z, y).
Axes of the slice: x: 4, y: 4, z: 4, core: 2. Of those that a mesh axis runs over, the one named last changes fastest.
Arguments:
- coherency: bfloat16 [8, 1024, 8192], P(None, 'bl', 'freq'), may hold values from -2 to 2
- visibility: float32 [8, 1024, 256], P(None, 'bl', 'freq'), may hold values from -6 to 6
- span_lengths: int32 [1024], P('bl'), may hold values from 1 to 8, 4096 in all
- station_pairs: int32 [2, 1024], P(None, 'bl'), may hold values from 0 to 61, as said below
- jones_field: float32 [8, 64, 8192], P(None, 'bl', 'freq'), may hold values from -1.2 to 2.2
- dual_field: float32 [8, 64, 8192], P(None, 'bl', 'freq'), may hold values from -6 to 6
- consensus_coeffs: float32 [4, 8, 64, 32], P(None, None, 'bl'), may hold values from -6 to 6
Outputs:
- jones_next: float32 [8, 64, 8192], P(None, 'bl', 'freq')
- dual_next: float32 [8, 64, 8192], P(None, 'bl', 'freq')
- consensus_next: float32 [4, 8, 64, 32], P(None, None, 'bl')
The draws below stay inside these ranges and needn't reach their ends.
Inputs may be any that keep to these rules, and one draw needn't show every extreme that they name: `station_pairs`: the two stations of a row differ; station numbers stay under 62.
All inputs are finite; a program needn't handle non-finite values. No bound on the sum of `span_lengths` on one device may be relied on, other than what follows from the above.
Results may differ from the reference program's by a relative error of at most 0.0003.
Values sent between devices are 32-bit elements; how exact they have to be, the bound alone decides.
A program may use at most 64 MiB of HBM per device.

```python
import math
import jax
import jax.numpy as jnp
import numpy as np
from jax import lax

STATIONS = 62
SLOTS = 64
DIRS = 32
CHANS = 256
ROWS = 1024
ITERS = 2
NTERMS = 4
MOST = 8


def draw_station_pairs(key, part):
    key = jax.random.fold_in(key, 11)
    first_key, offset_key = jax.random.split(key)
    left_side = jax.random.randint(first_key, (ROWS,), 0, STATIONS)
    offset = jax.random.randint(offset_key, (ROWS,), 1, STATIONS)
    right_side = (left_side + offset) % STATIONS
    left_side = left_side.at[0].set(0)
    right_side = right_side.at[0].set(STATIONS - 1)
    return jnp.stack([left_side, right_side]).astype(jnp.int32)


def draw_jones_field(key, part):
    key = jax.random.fold_in(key, 5)
    shape = (8, SLOTS, CHANS * DIRS)
    noise = 0.3 * jnp.clip(jax.random.normal(key, shape, jnp.float32), -4.0, 4.0)
    component = lax.broadcasted_iota(jnp.int32, shape, 0)
    identity = jnp.where((component == 0) | (component == 3), 1.0, 0.0).astype(jnp.float32)
    return (identity + noise).astype(jnp.float32)


def block_scale(key, extent, shards, smallest, largest):
    level = 1.0
    for axis_at, parts in shards:
        steps = jax.random.uniform(jax.random.fold_in(jax.random.fold_in(key, 6), axis_at), (parts,), jnp.float32, smallest / len(shards), largest / len(shards))
        level = level * jnp.repeat(jnp.exp(steps), extent[axis_at] // parts).reshape((-1,) + (1,) * (len(extent) - 1 - axis_at))
    return level


def split_up(amount, total, bound, lean):
    portions = [(1 << 20) // math.isqrt(rank ** lean) + 1 for rank in range(2, amount + 1)]
    rest, counts = total - bound - (amount - 1), [1] * (amount - 1)
    while rest > 0:
        candidates = [i for i in range(amount - 1) if counts[i] < bound]
        pool, left = sum([portions[i] for i in candidates]), rest
        for i in candidates:
            addition = min(bound - counts[i], max(1, left * portions[i] // pool), rest)
            counts[i] = counts[i] + addition
            rest = rest - addition
    return np.array([bound] + counts)


def ragged_sizes(stream_key, amount, total, bound, skew):
    if amount == 2:
        one = jax.random.randint(stream_key, (), max(1, total - bound), min(bound, total - 1) + 1)
        return jnp.stack([one, total - one])
    lengths = jnp.asarray(split_up(amount, total, bound, skew), jnp.int32)
    twos = (amount - 1) // 2
    source_of, receiver = lengths[1:1 + 2 * twos:2], lengths[2:2 + 2 * twos:2]
    room = jnp.minimum(source_of - 1, bound - receiver)
    passed = jax.random.randint(jax.random.fold_in(stream_key, 1), (twos,), 0, 1 << 20) % (room + 1)
    lengths = lengths.at[1:1 + 2 * twos:2].set(source_of - passed).at[2:2 + 2 * twos:2].set(receiver + passed)
    return lengths[jax.random.permutation(jax.random.fold_in(stream_key, 2), amount)]


def scatter_about(key, dims, width, bound, cuts=(), kind=jnp.bfloat16):
    values = jax.random.normal(key, dims, jnp.float32) * width
    if len(cuts) > 0:
        values = block_scale(key, dims, cuts, -0.22, 0.18) * values
    return jnp.clip(values, min=-bound, max=bound).astype(kind)


def setup_inputs(seed: int = 0) -> dict:
    arg_keys = jax.random.split(jax.random.key(seed), 8)
    return {
        "coherency": scatter_about(arg_keys[0], (8, ROWS, CHANS * DIRS), ((2 * DIRS) ** -0.5), 2.0, ((1, 16), (2, 8))),
        "visibility": scatter_about(arg_keys[1], (8, ROWS, CHANS), 1.0, 6.0, ((1, 16), (2, 8)), jnp.float32),
        "span_lengths": ragged_sizes(arg_keys[2], ROWS, 4 * ROWS, MOST, 2).astype(jnp.int32),
        "station_pairs": draw_station_pairs(jax.random.fold_in(arg_keys[7], 71), 0),
        "jones_field": draw_jones_field(jax.random.fold_in(arg_keys[7], 71), 0),
        "dual_field": scatter_about(arg_keys[5], (8, SLOTS, CHANS * DIRS), 0.5, 6.0, ((1, 16), (2, 8)), jnp.float32),
        "consensus_coeffs": scatter_about(arg_keys[6], (NTERMS, 8, SLOTS, DIRS), 0.5, 6.0, ((2, 16),), jnp.float32),
    }


penalty = 4.0
damping = 0.5


def complex_product(first_mat, second_mat):
    real_a, imag_a = first_mat[0:4], first_mat[4:8]
    real_b, imag_b = second_mat[0:4], second_mat[4:8]
    real_out = []
    imag_out = []
    for i in range(2):
        for j in range(2):
            real_out.append(real_a[2 * i] * real_b[j] + real_a[2 * i + 1] * real_b[2 + j]
                            - imag_a[2 * i] * imag_b[j] - imag_a[2 * i + 1] * imag_b[2 + j])
            imag_out.append(real_a[2 * i] * imag_b[j] + real_a[2 * i + 1] * imag_b[2 + j]
                            + imag_a[2 * i] * real_b[j] + imag_a[2 * i + 1] * real_b[2 + j])
    return jnp.stack(real_out + imag_out)


def adjoint(matrix):
    return jnp.stack([matrix[0], matrix[2], matrix[1], matrix[3],
                      -matrix[4], -matrix[6], -matrix[5], -matrix[7]])


def hermitian_square(matrix):
    top = matrix[0] ** 2 + matrix[1] ** 2 + matrix[4] ** 2 + matrix[5] ** 2
    bottom = matrix[2] ** 2 + matrix[3] ** 2 + matrix[6] ** 2 + matrix[7] ** 2
    cross_real = matrix[0] * matrix[2] + matrix[4] * matrix[6] + matrix[1] * matrix[3] + matrix[5] * matrix[7]
    cross_imag = matrix[4] * matrix[2] - matrix[0] * matrix[6] + matrix[5] * matrix[3] - matrix[1] * matrix[7]
    return jnp.stack([top, bottom, cross_real, cross_imag])


def solve_step(rhs_field, normal, shift_value):
    top = normal[0] + shift_value
    bottom = normal[1] + shift_value
    cross_real = normal[2]
    cross_imag = normal[3]
    determinant = top * bottom - cross_real * cross_real - cross_imag * cross_imag
    nothing = jnp.zeros_like(top)
    inverse = jnp.stack([bottom, -cross_real, -cross_real, top,
                         nothing, -cross_imag, cross_imag, nothing]) / determinant
    return complex_product(rhs_field, inverse)


def row_terms(jones_left, jones_right, coherency, visibility, weight, group):
    coherent = coherency.astype(jnp.float32)
    applied = complex_product(coherent, adjoint(jones_right))
    model = complex_product(jones_left, applied)
    shape = model.shape
    grouped = model.reshape(shape[:-1] + (shape[-1] // group, group))
    model_sum = jnp.sum(grouped, axis=-1)
    misfit = jnp.broadcast_to((visibility - model_sum)[..., None], grouped.shape).reshape(shape)
    outer = complex_product(jones_left, coherent)
    left_terms = jnp.concatenate([complex_product(misfit, adjoint(applied)), hermitian_square(applied)]) * weight
    right_terms = jnp.concatenate([complex_product(adjoint(misfit), outer), hermitian_square(adjoint(outer))]) * weight
    return left_terms, right_terms


def cosine_basis(nterms, total, first, count):
    channel = (first + jnp.arange(count, dtype=jnp.int32)).astype(jnp.float32)
    order = jnp.arange(nterms, dtype=jnp.int32).astype(jnp.float32)
    basis = jnp.cos(jnp.pi * order[:, None] * (channel[None, :] + 0.5) / total)
    norms = jnp.where(order == 0.0, 1.0 * total, 0.5 * total).astype(jnp.float32)
    return basis, norms


def collect_rows(terms, stations):
    moved = jnp.moveaxis(terms, 1, 0)
    summed = jax.ops.segment_sum(moved, stations, num_segments=SLOTS)
    return jnp.moveaxis(summed, 0, 1)


def reference(coherency, visibility, span_lengths, station_pairs, jones_field, dual_field, consensus_coeffs):
    highest = lax.Precision.HIGHEST
    basis, norms = cosine_basis(NTERMS, CHANS, 0, CHANS)
    dual_four = dual_field.reshape(8, SLOTS, CHANS, DIRS)
    jones_four = jones_field.reshape(8, SLOTS, CHANS, DIRS)
    coher_four = coherency.reshape(8, ROWS, CHANS, DIRS)
    prior = penalty * jnp.einsum("mf,mcsk->csfk", basis, consensus_coeffs, precision=highest) - dual_four
    weight = span_lengths.astype(jnp.float32)[:, None]
    left_ids = station_pairs[0]
    right_ids = station_pairs[1]

    def one_channel(index):
        current = lax.dynamic_slice_in_dim(jones_four, index, 1, 2)[:, :, 0]
        coher_block = lax.dynamic_slice_in_dim(coher_four, index, 1, 2)[:, :, 0]
        vis_block = lax.dynamic_slice_in_dim(visibility, index, 1, 2)
        prior_block = lax.dynamic_slice_in_dim(prior, index, 1, 2)[:, :, 0]
        for step in range(ITERS):
            left_rows = jnp.take(current, left_ids, axis=1)
            right_rows = jnp.take(current, right_ids, axis=1)
            left_terms, right_terms = row_terms(left_rows, right_rows, coher_block, vis_block, weight, DIRS)
            summed = collect_rows(left_terms, left_ids) + collect_rows(right_terms, right_ids)
            rhs_field = summed[:8] + prior_block - penalty * current
            current = current + damping * solve_step(rhs_field, summed[8:], penalty)
        return current

    solved = lax.map(one_channel, jnp.arange(CHANS, dtype=jnp.int32))
    jones_next_four = jnp.transpose(solved, (1, 2, 0, 3))
    blended = jones_next_four + dual_four / penalty
    consensus_next = jnp.einsum("mf,csfk->mcsk", basis / norms[:, None], blended, precision=highest)
    smooth = jnp.einsum("mf,mcsk->csfk", basis, consensus_next, precision=highest)
    dual_next = dual_four + penalty * (jones_next_four - smooth)
    jones_next = jones_next_four.reshape(8, SLOTS, CHANS * DIRS)
    return jones_next, dual_next.reshape(8, SLOTS, CHANS * DIRS), consensus_next
```

```python
import functools

import jax
import jax.numpy as jnp
import numpy as np
from jax import lax
from jax.experimental import pallas as pl
from jax.experimental.pallas import tpu as pltpu
from jax.sharding import PartitionSpec as P

CHANS = 256
ITERS = 2
NTERMS = 4
PENALTY = 4.0
DAMPING = 0.5

RING = 4
PEERS = 16
FREQS = 8
STAGES = 2
QUARTERS = 4
BAND = 16
DIRS = 32
SLOTS = 64
ROWS = PEERS * BAND
HEAD = 24
GROUP = 4

MESH = pl.DeviceIdType.MESH
F32 = jnp.float32
BF16 = jnp.bfloat16


def basis_table():
    channel = np.arange(CHANS, dtype=np.float64) + 0.5
    order = np.arange(NTERMS, dtype=np.float64)
    return np.cos(np.pi * order[:, None] * channel[None, :] / CHANS).astype(np.float32)


def norm_of(term):
    return float(CHANS) if term == 0 else 0.5 * CHANS


def product(a, b):
    real, imag = [], []
    for i in range(2):
        for j in range(2):
            real.append(
                a[2 * i] * b[j]
                + a[2 * i + 1] * b[2 + j]
                - a[4 + 2 * i] * b[4 + j]
                - a[4 + 2 * i + 1] * b[4 + 2 + j]
            )
            imag.append(
                a[2 * i] * b[4 + j]
                + a[2 * i + 1] * b[4 + 2 + j]
                + a[4 + 2 * i] * b[j]
                + a[4 + 2 * i + 1] * b[2 + j]
            )
    return real + imag


def product_adjoint(a, b):
    real, imag = [], []
    for i in range(2):
        for j in range(2):
            real.append(
                a[2 * i] * b[2 * j]
                + a[2 * i + 1] * b[2 * j + 1]
                + a[4 + 2 * i] * b[4 + 2 * j]
                + a[4 + 2 * i + 1] * b[4 + 2 * j + 1]
            )
            imag.append(
                a[4 + 2 * i] * b[2 * j]
                + a[4 + 2 * i + 1] * b[2 * j + 1]
                - a[2 * i] * b[4 + 2 * j]
                - a[2 * i + 1] * b[4 + 2 * j + 1]
            )
    return real + imag


def adjoint_product(a, b):
    real, imag = [], []
    for i in range(2):
        for j in range(2):
            real.append(
                a[i] * b[j] + a[2 + i] * b[2 + j] + a[4 + i] * b[4 + j] + a[6 + i] * b[6 + j]
            )
            imag.append(
                a[i] * b[4 + j] + a[2 + i] * b[6 + j] - a[4 + i] * b[j] - a[6 + i] * b[2 + j]
            )
    return real + imag


def square_right(a):
    top = a[0] * a[0] + a[1] * a[1] + a[4] * a[4] + a[5] * a[5]
    bottom = a[2] * a[2] + a[3] * a[3] + a[6] * a[6] + a[7] * a[7]
    real = a[0] * a[2] + a[4] * a[6] + a[1] * a[3] + a[5] * a[7]
    imag = a[4] * a[2] - a[0] * a[6] + a[5] * a[3] - a[1] * a[7]
    return [top, bottom, real, imag]


def square_left(a):
    return square_right([a[0], a[2], a[1], a[3], -a[4], -a[6], -a[5], -a[7]])


def halves(x):
    high = x.astype(BF16)
    return high, (x - high.astype(F32)).astype(BF16)


def lane_block(shape):
    return lax.shift_right_logical(lax.broadcasted_iota(jnp.int32, shape, len(shape) - 1), 5)


def swap_blocks(x):
    block = lane_block(x[0].shape)
    left = block < 2
    even = (block & 1) == 0
    halfway = [None] * 4
    for low in range(2):
        first, second = x[low], x[2 + low]
        halfway[low] = jnp.where(left, first, pltpu.roll(second, 64, 1))
        halfway[2 + low] = jnp.where(left, pltpu.roll(first, 64, 1), second)
    out = [None] * 4
    for high in range(2):
        first, second = halfway[2 * high], halfway[2 * high + 1]
        out[2 * high] = jnp.where(even, first, pltpu.roll(second, 32, 1))
        out[2 * high + 1] = jnp.where(even, pltpu.roll(first, 96, 1), second)
    return out


def spread_lanes(x):
    x = x + pltpu.roll(x, 64, 1)
    return x + pltpu.roll(x, 32, 1)


def dot(a, b):
    return jnp.dot(a, b, preferred_element_type=F32)


def kernel(
    basis, coh, vis, span, pairs, jones, dual, cons,
    jones_out, dual_out, cons_out,
    csend, crecv, hsend, hrecv, rsend, rrecv, psend, precv,
    meta, const, dual_t, jpq, vis_x, terms, ohg, ohs, jrhs, ones_blk, field, prior,
    csend_sem, crecv_sem, hsend_sem, hrecv_sem, rsend_sem, rrecv_sem, psend_sem, precv_sem, own_sem,
):
    me = lax.axis_index("bl")
    fr = lax.axis_index("freq")
    z, y = me // RING, me % RING
    first_chan = fr * (CHANS // FREQS)

    def ahead(j):
        return lax.rem(z + j // RING, RING) * RING + lax.rem(y + j % RING, RING)

    def behind(j):
        return lax.rem(z + RING - j // RING, RING) * RING + lax.rem(y + RING - j % RING, RING)

    def freq_ahead(g):
        return lax.rem(fr + g, FREQS)

    barrier = pltpu.get_barrier_semaphore()
    for j in range(1, PEERS):
        pl.semaphore_signal(barrier, inc=1, device_id={"bl": ahead(j)}, device_id_type=MESH)
    for g in range(1, FREQS):
        pl.semaphore_signal(barrier, inc=1, device_id={"freq": freq_ahead(g)}, device_id_type=MESH)

    def basis_at(term, chan):
        return basis[term, first_chan + chan]


    def c_copy(t, j):
        return pltpu.make_async_remote_copy(
            src_ref=csend.at[t, ahead(j)], dst_ref=crecv.at[t, j],
            send_sem=csend_sem.at[t, j], recv_sem=crecv_sem.at[t, j],
            device_id={"bl": ahead(j)}, device_id_type=MESH,
        )

    def h_copy(t, j):
        return pltpu.make_async_remote_copy(
            src_ref=hsend.at[t, ahead(j)], dst_ref=hrecv.at[t, j],
            send_sem=hsend_sem.at[t, j], recv_sem=hrecv_sem.at[t, j],
            device_id={"bl": ahead(j)}, device_id_type=MESH,
        )

    def r_copy(t, j):
        return pltpu.make_async_remote_copy(
            src_ref=rsend.at[t, j], dst_ref=rrecv.at[t, me],
            send_sem=rsend_sem.at[t, j], recv_sem=rrecv_sem.at[t, j],
            device_id={"bl": behind(j)}, device_id_type=MESH,
        )

    def p_copy(g):
        return pltpu.make_async_remote_copy(
            src_ref=psend, dst_ref=precv.at[fr],
            send_sem=psend_sem.at[g], recv_sem=precv_sem.at[g],
            device_id={"freq": freq_ahead(g)}, device_id_type=MESH,
        )


    for m in range(NTERMS):
        for s in range(4):
            const[m, :, DIRS * s : DIRS * s + DIRS] = cons[m, :, s, :]
    meta[...] = jnp.zeros_like(meta)
    meta[0:2, 0:64] = pairs[...].astype(F32)
    meta[2:3, 0:64] = span[...].astype(F32)
    vis_t = jnp.transpose(vis[...].reshape(8 * 64, 32))
    for t in range(STAGES):
        for d in range(PEERS):
            for i in range(4):
                hsend[t, d, 16 + i : 17 + i, :] = vis_t[
                    PEERS * t + d : PEERS * t + d + 1, 128 * i : 128 * i + 128
                ]
            hsend[t, d, 20:24, :] = meta[0:4, :]

    def build_head(t):
        for tile in range(4):
            lanes = pl.ds(128 * (4 * t + tile), 128)
            j_tile = swap_blocks([jones[:, s, lanes] for s in range(4)])
            d_tile = swap_blocks([dual[:, s, lanes] for s in range(4)])
            for a in range(4):
                d = 4 * tile + a
                chan = PEERS * t + d
                smooth = const[0] * basis_at(0, chan)
                for m in range(1, NTERMS):
                    smooth = smooth + const[m] * basis_at(m, chan)
                dual_t[chan] = d_tile[a]
                hsend[t, d, 0:8, :] = j_tile[a]
                hsend[t, d, 8:16, :] = PENALTY * smooth - d_tile[a]

    def build_c(t):
        def one(c, _):
            for tile in range(4):
                lanes = pl.ds(128 * (4 * t + tile), 128)
                parts = swap_blocks(
                    [coh[c, BAND * q : BAND * q + BAND, lanes].astype(F32) for q in range(QUARTERS)]
                )
                for a in range(4):
                    csend[t, 4 * tile + a, c] = parts[a]
            return 0

        lax.fori_loop(0, 8, one, 0)

    def own_copies(t):
        return (
            pltpu.make_async_copy(hsend.at[t, me], hrecv.at[t, 0], own_sem.at[2 * t]),
            pltpu.make_async_copy(csend.at[t, me], crecv.at[t, 0], own_sem.at[2 * t + 1]),
        )

    def send_all(t):
        for copy in own_copies(t):
            copy.start()

        def head(j, _):
            h_copy(t, j).start()
            return 0

        def body(j, _):
            c_copy(t, j).start()
            return 0

        lax.fori_loop(1, PEERS, head, 0)
        lax.fori_loop(1, PEERS, body, 0)

    build_head(0)
    build_c(0)
    pl.semaphore_wait(barrier, PEERS - 1 + FREQS - 1)
    send_all(0)
    build_head(1)
    build_c(1)
    send_all(1)

    row_block = lax.shift_right_logical(lax.broadcasted_iota(jnp.int32, (256, 128), 0), 5) & 3
    ones_blk[...] = jnp.where(row_block == lane_block((256, 128)), 1.0, 0.0).astype(BF16)

    band_mask = (lax.broadcasted_iota(jnp.int32, (BAND, 128), 1) & (BAND - 1)) == (
        lax.broadcasted_iota(jnp.int32, (BAND, 128), 0)
    )

    def banded(t, row):
        return jnp.concatenate(
            [
                jnp.where(band_mask, jnp.broadcast_to(hrecv[t, j, row : row + 1, :], (BAND, 128)), 0.0)
                for j in range(PEERS)
            ],
            axis=0,
        )

    def build_onehots():
        source = lax.broadcasted_iota(jnp.int32, (128, 256), 0)
        target = lax.broadcasted_iota(jnp.int32, (128, 256), 1)
        expand = jnp.where(
            lax.shift_right_logical(source, 4) == lax.shift_right_logical(target, 6), 1.0, 0.0
        ).astype(BF16)
        position = lax.broadcasted_iota(jnp.int32, (1, 256), 1) & (SLOTS - 1)
        j = position & (PEERS - 1)
        owner_z = (z + RING - lax.shift_right_logical(j, 2)) & (RING - 1)
        owner_y = (y + RING - (j & 3)) & (RING - 1)
        label = 4 * (owner_z * RING + owner_y) + lax.shift_right_logical(position, 4)
        label = label.astype(F32)
        weight = dot(banded(0, 22).astype(BF16), expand)
        for side in range(2):
            station = dot(banded(0, 20 + side).astype(BF16), expand)
            hit = station == label
            onehot = jnp.where(hit, 1.0, 0.0).astype(BF16)
            ohg[ROWS * side : ROWS * side + ROWS, 0:256] = onehot
            ohg[ROWS * side : ROWS * side + ROWS, 256:512] = onehot
            weighted = jnp.transpose(jnp.where(hit, weight, 0.0)).astype(BF16)
            ohs[:, 512 * side : 512 * side + 256] = weighted
            ohs[:, 512 * side + 256 : 512 * side + 512] = weighted

    def build_visibility(t):
        source = lax.broadcasted_iota(jnp.int32, (256, 256), 0) & 127
        target = lax.broadcasted_iota(jnp.int32, (256, 256), 1)
        expand = jnp.where(
            lax.shift_right_logical(source, 4) == lax.shift_right_logical(target, 5), 1.0, 0.0
        ).astype(BF16)
        for i in range(4):
            high, low = halves(banded(t, 16 + i))
            out = dot(jnp.concatenate([high, low], axis=1), expand)
            vis_x[2 * i] = out[:, 0:128]
            vis_x[2 * i + 1] = out[:, 128:256]

    def build_field(t):
        block = lane_block((PEERS, 128))
        for c in range(16):
            flat = jnp.concatenate([hrecv[t, j, c : c + 1, :] for j in range(PEERS)], axis=0)
            target = field if c < 8 else prior
            for s in range(4):
                target[c % 8, PEERS * s : PEERS * s + PEERS] = spread_lanes(
                    jnp.where(block == s, flat, 0.0)
                )

    def gather():
        block = lane_block((SLOTS, 128))
        for c in range(8):
            for at, part in enumerate(halves(field[c])):
                for q in range(QUARTERS):
                    first = 256 * at + SLOTS * q
                    jrhs[first : first + SLOTS, 128 * c : 128 * c + 128] = jnp.where(
                        block == q, part.astype(F32), 0.0
                    ).astype(BF16)
        for c in range(4):
            jpq[:, 256 * c : 256 * c + 256] = dot(ohg[...], jrhs[:, 256 * c : 256 * c + 256])

    def process(t, group):
        size = GROUP * BAND
        first = pl.multiple_of(group * size, size)
        rows = pl.ds(first, size)
        sources = pl.ds(group * GROUP, GROUP)
        coherent = [crecv[t, sources, c].reshape(size, 128) for c in range(8)]
        left = [jpq[rows, 128 * c : 128 * c + 128] for c in range(8)]
        right = [jpq[pl.ds(ROWS + first, size), 128 * c : 128 * c + 128] for c in range(8)]
        applied = product_adjoint(coherent, right)
        model = product(left, applied)
        outer = product(left, coherent)
        split = [jnp.concatenate(halves(x), axis=1) for x in model]
        total = dot(jnp.concatenate(split, axis=0), ones_blk[...])
        misfit = [vis_x[c, rows, :] - total[size * c : size * c + size] for c in range(8)]
        for side in range(2):
            if side == 0:
                out = product_adjoint(misfit, applied) + square_right(applied)
            else:
                out = adjoint_product(misfit, outer) + square_left(outer)
            for c in range(12):
                for at, part in enumerate(halves(out[c])):
                    terms[pl.ds(ROWS * (2 * side + at) + first, size), 128 * c : 128 * c + 128] = part

    def solve():
        block = lane_block((SLOTS, 128))
        sums = []
        for pair in range(6):
            res = dot(ohs[...], terms[:, 256 * pair : 256 * pair + 256])
            for half in range(2):
                part = res[:, 128 * half : 128 * half + 128]
                total = jnp.where(block == 0, part[0:SLOTS], 0.0)
                for q in range(1, QUARTERS):
                    total = jnp.where(block == q, part[SLOTS * q : SLOTS * q + SLOTS], total)
                sums.append(spread_lanes(total))
        current = [field[c] for c in range(8)]
        rhs = [sums[c] + prior[c] - PENALTY * current[c] for c in range(8)]
        top = sums[8] + PENALTY
        bottom = sums[9] + PENALTY
        real, imag = sums[10], sums[11]
        scale = DAMPING / (top * bottom - real * real - imag * imag)
        for i in range(2):
            a, b = rhs[2 * i], rhs[2 * i + 1]
            c, d = rhs[4 + 2 * i], rhs[4 + 2 * i + 1]
            field[2 * i] = current[2 * i] + scale * (a * bottom - b * real - d * imag)
            field[2 * i + 1] = current[2 * i + 1] + scale * (b * top - a * real + c * imag)
            field[4 + 2 * i] = current[4 + 2 * i] + scale * (c * bottom - d * real + b * imag)
            field[5 + 2 * i] = current[5 + 2 * i] + scale * (d * top - c * real - a * imag)

    def send_back(t):
        block = lane_block((PEERS, 128))
        for c in range(8):
            whole = field[c]
            flat = jnp.where(block == 0, whole[0:PEERS], 0.0)
            for s in range(1, 4):
                flat = jnp.where(block == s, whole[PEERS * s : PEERS * s + PEERS], flat)
            for j in range(PEERS):
                rsend[t, j, c : c + 1, :] = flat[j : j + 1]
        rrecv[t, me] = rsend[t, 0]
        for j in range(1, PEERS):
            r_copy(t, j).start()

    def wait_each(copy, t):
        def one(j, _):
            copy(t, j).wait()
            return 0

        lax.fori_loop(1, PEERS, one, 0)

    for t in range(STAGES):
        own = own_copies(t)
        own[0].wait()
        wait_each(h_copy, t)
        if t == 0:
            build_onehots()
        build_visibility(t)
        build_field(t)
        gather()
        own[1].wait()

        def first_sweep(group, _):
            def arrive(j, _):
                c_copy(t, j).wait()
                return 0

            lax.fori_loop(jnp.maximum(group * GROUP, 1), (group + 1) * GROUP, arrive, 0)
            process(t, group)
            return 0

        def later_sweep(group, _):
            process(t, group)
            return 0

        lax.fori_loop(0, PEERS // GROUP, first_sweep, 0)
        solve()
        for _ in range(1, ITERS):
            gather()
            lax.fori_loop(0, PEERS // GROUP, later_sweep, 0)
            solve()
        send_back(t)

    projected = [jnp.zeros((8, 128), F32) for _ in range(NTERMS)]
    for t in range(STAGES):
        wait_each(r_copy, t)
        for d in range(PEERS):
            chan = PEERS * t + d
            blended = rrecv[t, d] + dual_t[chan] * (1.0 / PENALTY)
            for m in range(NTERMS):
                projected[m] = projected[m] + blended * (basis_at(m, chan) * (1.0 / norm_of(m)))
    for m in range(NTERMS):
        psend[m] = projected[m]
        precv[fr, m] = projected[m]
    for g in range(1, FREQS):
        p_copy(g).start()
    for t in range(STAGES):
        for tile in range(4):
            lanes = pl.ds(128 * (4 * t + tile), 128)
            parts = swap_blocks([rrecv[t, 4 * tile + a] for a in range(4)])
            for s in range(4):
                jones_out[:, s, lanes] = parts[s]
    for g in range(1, FREQS):
        p_copy(g).wait()
    block = lane_block((8, 128))
    smooth = []
    for m in range(NTERMS):
        total = precv[0, m]
        for g in range(1, FREQS):
            total = total + precv[g, m]
        for s in range(4):
            cons_out[m, :, s, :] = total[:, DIRS * s : DIRS * s + DIRS]
        smooth.append([spread_lanes(jnp.where(block == s, total, 0.0)) for s in range(4)])
    lane = lane_block((1, 128))
    for tile in range(8):
        lanes = pl.ds(128 * tile, 128)
        rows = []
        for m in range(NTERMS):
            row = jnp.full((1, 128), basis_at(m, 4 * tile), F32)
            for a in range(1, 4):
                row = jnp.where(lane == a, basis_at(m, 4 * tile + a), row)
            rows.append(row)
        for s in range(4):
            fitted = rows[0] * smooth[0][s]
            for m in range(1, NTERMS):
                fitted = fitted + rows[m] * smooth[m][s]
            dual_out[:, s, lanes] = dual[:, s, lanes] + PENALTY * (jones_out[:, s, lanes] - fitted)


def shards(coherency, visibility, span_lengths, station_pairs, jones_field, dual_field, consensus):
    vmem = pl.BlockSpec(memory_space=pltpu.VMEM)
    smem = pl.BlockSpec(memory_space=pltpu.SMEM)
    dma = pltpu.SemaphoreType.DMA
    return pl.pallas_call(
        kernel,
        out_shape=(
            jax.ShapeDtypeStruct(jones_field.shape, F32),
            jax.ShapeDtypeStruct(dual_field.shape, F32),
            jax.ShapeDtypeStruct(consensus.shape, F32),
        ),
        in_specs=[smem] + [vmem] * 7,
        out_specs=(vmem,) * 3,
        scratch_shapes=[
            pltpu.VMEM((STAGES, PEERS, 8, BAND, 128), F32),
            pltpu.VMEM((STAGES, PEERS, 8, BAND, 128), F32),
            pltpu.VMEM((STAGES, PEERS, HEAD, 128), F32),
            pltpu.VMEM((STAGES, PEERS, HEAD, 128), F32),
            pltpu.VMEM((STAGES, PEERS, 8, 128), F32),
            pltpu.VMEM((STAGES, PEERS, 8, 128), F32),
            pltpu.VMEM((NTERMS, 8, 128), F32),
            pltpu.VMEM((FREQS, NTERMS, 8, 128), F32),
            pltpu.VMEM((8, 128), F32),
            pltpu.VMEM((NTERMS, 8, 128), F32),
            pltpu.VMEM((STAGES * PEERS, 8, 128), F32),
            pltpu.VMEM((2 * ROWS, 8 * 128), F32),
            pltpu.VMEM((8, ROWS, 128), F32),
            pltpu.VMEM((4 * ROWS, 12 * 128), BF16),
            pltpu.VMEM((2 * ROWS, 512), BF16),
            pltpu.VMEM((QUARTERS * SLOTS, 4 * ROWS), BF16),
            pltpu.VMEM((2 * QUARTERS * SLOTS, 8 * 128), BF16),
            pltpu.VMEM((256, 128), BF16),
            pltpu.VMEM((8, SLOTS, 128), F32),
            pltpu.VMEM((8, SLOTS, 128), F32),
            dma((STAGES, PEERS)),
            dma((STAGES, PEERS)),
            dma((STAGES, PEERS)),
            dma((STAGES, PEERS)),
            dma((STAGES, PEERS)),
            dma((STAGES, PEERS)),
            dma((FREQS,)),
            dma((FREQS,)),
            dma((2 * STAGES,)),
        ],
        compiler_params=pltpu.CompilerParams(
            collective_id=0, has_side_effects=True, vmem_limit_bytes=40 * 2**20
        ),
        name="calibrate",
    )(
        jnp.asarray(basis_table()),
        coherency,
        visibility,
        span_lengths.reshape(1, -1),
        station_pairs,
        jones_field,
        dual_field,
        consensus,
    )


def solution(mesh):
    in_specs = (
        P(None, "bl", "freq"),
        P(None, "bl", "freq"),
        P("bl"),
        P(None, "bl"),
        P(None, "bl", "freq"),
        P(None, "bl", "freq"),
        P(None, None, "bl", None),
    )
    out_specs = (P(None, "bl", "freq"), P(None, "bl", "freq"), P(None, None, "bl", None))
    return jax.shard_map(shards, mesh=mesh, in_specs=in_specs, out_specs=out_specs, check_vma=False)
```

```python
import functools

import jax
import jax.numpy as jnp
import numpy as np
from jax import lax
from jax.experimental import pallas as pl
from jax.experimental.pallas import tpu as pltpu
from jax.sharding import PartitionSpec as P

CHANS = 256
ITERS = 2
NTERMS = 4
PENALTY = 4.0
DAMPING = 0.5

RING = 4
PEERS = 16
FREQS = 8
STAGES = 2
QUARTERS = 4
BAND = 16
DIRS = 32
SLOTS = 64
ROWS = PEERS * BAND
HEAD = 24
GROUP = 4
OWN = 4

MESH = pl.DeviceIdType.MESH
F32 = jnp.float32
BF16 = jnp.bfloat16


def basis_table():
    channel = np.arange(CHANS, dtype=np.float64) + 0.5
    order = np.arange(NTERMS, dtype=np.float64)
    return np.cos(np.pi * order[:, None] * channel[None, :] / CHANS).astype(np.float32)


def norm_of(term):
    return float(CHANS) if term == 0 else 0.5 * CHANS


def product(a, b):
    real, imag = [], []
    for i in range(2):
        for j in range(2):
            real.append(
                a[2 * i] * b[j]
                + a[2 * i + 1] * b[2 + j]
                - a[4 + 2 * i] * b[4 + j]
                - a[4 + 2 * i + 1] * b[4 + 2 + j]
            )
            imag.append(
                a[2 * i] * b[4 + j]
                + a[2 * i + 1] * b[4 + 2 + j]
                + a[4 + 2 * i] * b[j]
                + a[4 + 2 * i + 1] * b[2 + j]
            )
    return real + imag


def product_adjoint(a, b):
    real, imag = [], []
    for i in range(2):
        for j in range(2):
            real.append(
                a[2 * i] * b[2 * j]
                + a[2 * i + 1] * b[2 * j + 1]
                + a[4 + 2 * i] * b[4 + 2 * j]
                + a[4 + 2 * i + 1] * b[4 + 2 * j + 1]
            )
            imag.append(
                a[4 + 2 * i] * b[2 * j]
                + a[4 + 2 * i + 1] * b[2 * j + 1]
                - a[2 * i] * b[4 + 2 * j]
                - a[2 * i + 1] * b[4 + 2 * j + 1]
            )
    return real + imag


def adjoint_product(a, b):
    real, imag = [], []
    for i in range(2):
        for j in range(2):
            real.append(
                a[i] * b[j] + a[2 + i] * b[2 + j] + a[4 + i] * b[4 + j] + a[6 + i] * b[6 + j]
            )
            imag.append(
                a[i] * b[4 + j] + a[2 + i] * b[6 + j] - a[4 + i] * b[j] - a[6 + i] * b[2 + j]
            )
    return real + imag


def square_right(a):
    top = a[0] * a[0] + a[1] * a[1] + a[4] * a[4] + a[5] * a[5]
    bottom = a[2] * a[2] + a[3] * a[3] + a[6] * a[6] + a[7] * a[7]
    real = a[0] * a[2] + a[4] * a[6] + a[1] * a[3] + a[5] * a[7]
    imag = a[4] * a[2] - a[0] * a[6] + a[5] * a[3] - a[1] * a[7]
    return [top, bottom, real, imag]


def square_left(a):
    return square_right([a[0], a[2], a[1], a[3], -a[4], -a[6], -a[5], -a[7]])


def halves(x):
    high = x.astype(BF16)
    return high, (x - high.astype(F32)).astype(BF16)


def lane_block(shape):
    return lax.shift_right_logical(lax.broadcasted_iota(jnp.int32, shape, len(shape) - 1), 5)


def swap_blocks(x):
    block = lane_block(x[0].shape)
    left = block < 2
    even = (block & 1) == 0
    halfway = [None] * 4
    for low in range(2):
        first, second = x[low], x[2 + low]
        halfway[low] = jnp.where(left, first, pltpu.roll(second, 64, 1))
        halfway[2 + low] = jnp.where(left, pltpu.roll(first, 64, 1), second)
    out = [None] * 4
    for high in range(2):
        first, second = halfway[2 * high], halfway[2 * high + 1]
        out[2 * high] = jnp.where(even, first, pltpu.roll(second, 32, 1))
        out[2 * high + 1] = jnp.where(even, pltpu.roll(first, 96, 1), second)
    return out


def spread_lanes(x):
    x = x + pltpu.roll(x, 64, 1)
    return x + pltpu.roll(x, 32, 1)


def dot(a, b):
    return jnp.dot(a, b, preferred_element_type=F32)


def basis_at(basis, term, chan):
    return basis[term, lax.axis_index("freq") * (CHANS // FREQS) + chan]


def offset(group, i):
    low, high = i % 2, i // 2
    sign = 1 + 2 * high
    if group == 0:
        return 2 * (1 - low) + sign * low, sign * (1 - low) + 2 * low
    if group == 1:
        return 2 * low, 2 * ((low + high) % 2)
    if group == 2:
        return 1 + 2 * low, 1 + 2 * ((low + high) % 2)
    return low * sign, (1 - low) * sign


def kernel(
    basis, coh_hbm, vis_hbm, span_hbm, pairs_hbm, jones_hbm, dual_hbm, cons_hbm,
    jones_out, lifted_out, smooth_out, rows_out,
    coh, vis, span, pairs, jones, dual, cons,
    perm, csend, crecv, hsend, hrecv, rsend, rrecv, psend, precv,
    meta, const, dual_t, jpq, vis_x, terms, ohg, ohs, jrhs, ones_blk, field, prior,
    csend_sem, crecv_sem, hsend_sem, hrecv_sem, rsend_sem, rrecv_sem, psend_sem, precv_sem, own_sem, in_sem,
):
    me = lax.axis_index("bl")
    fr = lax.axis_index("freq")
    z, y = me // RING, me % RING

    def ahead(group, i):
        dz, dy = offset(group, i)
        return lax.rem(z + dz, RING) * RING + lax.rem(y + dy, RING)

    def behind(group, i):
        dz, dy = offset(group, i)
        return lax.rem(z + RING - dz, RING) * RING + lax.rem(y + RING - dy, RING)

    def each_peer(step):
        for group in range(4):
            def one(i, _, group=group):
                step(group, i)
                return 0

            lax.fori_loop(1 if group == OWN // GROUP else 0, 4, one, 0)

    def freq_ahead(g):
        return lax.rem(fr + g, FREQS)


    loads = [
        pltpu.make_async_copy(source, target, in_sem.at[i])
        for i, (source, target) in enumerate(
            [
                (jones_hbm, jones), (dual_hbm, dual), (cons_hbm, cons), (vis_hbm, vis),
                (span_hbm, span), (pairs_hbm, pairs), (coh_hbm, coh),
            ]
        )
    ]
    for load in loads:
        load.start()

    barrier = pltpu.get_barrier_semaphore()
    each_peer(
        lambda group, i: pl.semaphore_signal(
            barrier, inc=1, device_id={"bl": ahead(group, i)}, device_id_type=MESH
        )
    )
    for g in range(1, FREQS):
        pl.semaphore_signal(barrier, inc=1, device_id={"freq": freq_ahead(g)}, device_id_type=MESH)

    def c_copy(t, group, i):
        j = 4 * group + i
        return pltpu.make_async_remote_copy(
            src_ref=csend.at[t, ahead(group, i)], dst_ref=crecv.at[t, j],
            send_sem=csend_sem.at[t, j], recv_sem=crecv_sem.at[t, j],
            device_id={"bl": ahead(group, i)}, device_id_type=MESH,
        )

    def h_copy(t, group, i):
        j = 4 * group + i
        return pltpu.make_async_remote_copy(
            src_ref=hsend.at[t, ahead(group, i)], dst_ref=hrecv.at[t, j],
            send_sem=hsend_sem.at[t, j], recv_sem=hrecv_sem.at[t, j],
            device_id={"bl": ahead(group, i)}, device_id_type=MESH,
        )

    def r_copy(t, group, i):
        j = 4 * group + i
        return pltpu.make_async_remote_copy(
            src_ref=rsend.at[t, j], dst_ref=rrecv.at[t, me],
            send_sem=rsend_sem.at[t, j], recv_sem=rrecv_sem.at[t, j],
            device_id={"bl": behind(group, i)}, device_id_type=MESH,
        )

    def arrived(t, j):
        return pltpu.make_async_remote_copy(
            src_ref=csend.at[t, j], dst_ref=crecv.at[t, j],
            send_sem=csend_sem.at[t, j], recv_sem=crecv_sem.at[t, j],
            device_id={"bl": ahead(3, 0)}, device_id_type=MESH,
        )

    def p_copy(g):
        return pltpu.make_async_remote_copy(
            src_ref=psend, dst_ref=precv.at[fr],
            send_sem=psend_sem.at[g], recv_sem=precv_sem.at[g],
            device_id={"freq": freq_ahead(g)}, device_id_type=MESH,
        )

    def own_copies(t):
        return (
            pltpu.make_async_copy(hsend.at[t, me], hrecv.at[t, OWN], own_sem.at[2 * t]),
            pltpu.make_async_copy(csend.at[t, me], crecv.at[t, OWN], own_sem.at[2 * t + 1]),
        )


    def lanes_of(u):
        return pl.ds(pl.multiple_of(128 * u, 128), 128)

    def build_head(u, _):
        t, tile = u // 4, u % 4
        lanes = lanes_of(u)
        j_tile = swap_blocks([jones[:, s, lanes] for s in range(4)])
        d_tile = swap_blocks([dual[:, s, lanes] for s in range(4)])
        for a in range(4):
            d = 4 * tile + a
            chan = 4 * u + a
            smooth = const[0] * basis_at(basis, 0, chan)
            for m in range(1, NTERMS):
                smooth = smooth + const[m] * basis_at(basis, m, chan)
            dual_t[chan] = d_tile[a]
            hsend[t, d, 0:8, :] = j_tile[a]
            hsend[t, d, 8:16, :] = PENALTY * smooth - d_tile[a]
        return 0

    def build_c(u, _):
        t, tile = u // 4, u % 4
        lanes = lanes_of(u)
        rows = jnp.concatenate(
            [coh[:, BAND * q : BAND * q + BAND, lanes].reshape(8 * BAND, 128) for q in range(QUARTERS)],
            axis=1,
        )
        out = dot(rows, perm[...])
        for a in range(4):
            csend[t, 4 * tile + a] = out[:, 128 * a : 128 * a + 128].reshape(8, BAND, 128)
        return 0

    at_row = lax.broadcasted_iota(jnp.int32, (128, 128), 0)
    apart = at_row - lax.broadcasted_iota(jnp.int32, (128, 128), 1)
    for a in range(4):
        for q in range(QUARTERS):
            hit = (apart == DIRS * (a - q)) & (lax.shift_right_logical(at_row, 5) == a)
            perm[128 * q : 128 * q + 128, 128 * a : 128 * a + 128] = jnp.where(hit, 1.0, 0.0).astype(BF16)

    for load in loads[:6]:
        load.wait()
    for m in range(NTERMS):
        for s in range(4):
            const[m, :, DIRS * s : DIRS * s + DIRS] = cons[m, :, s, :]
    meta[...] = jnp.zeros_like(meta)
    meta[0:2, 0:64] = pairs[...].astype(F32)
    meta[2:3, 0:64] = span[...].astype(F32)
    for t in range(STAGES):
        for i in range(4):
            pair = [vis[2 * i + half, PEERS * t : PEERS * t + PEERS, :] for half in range(2)]
            hsend[t, :, 16 + i, :] = jnp.concatenate(pair, axis=1)
        for d in range(PEERS):
            hsend[t, d, 20:24, :] = meta[0:4, :]
    lax.fori_loop(0, 8, build_head, 0)
    for load in loads[6:]:
        load.wait()
    lax.fori_loop(0, 4, build_c, 0)
    pl.semaphore_wait(barrier, PEERS - 1 + FREQS - 1)

    def send(t, _):
        for copy in own_copies(t):
            copy.start()
        each_peer(lambda group, i: h_copy(t, group, i).start())
        each_peer(lambda group, i: c_copy(t, group, i).start())

        @pl.when(t == 0)
        def _():
            lax.fori_loop(4, 8, build_c, 0)

        return 0

    lax.fori_loop(0, STAGES, send, 0)

    row_block = lax.shift_right_logical(lax.broadcasted_iota(jnp.int32, (256, 128), 0), 5) & 3
    ones_blk[...] = jnp.where(row_block == lane_block((256, 128)), 1.0, 0.0).astype(BF16)

    band_mask = (lax.broadcasted_iota(jnp.int32, (BAND, 128), 1) & (BAND - 1)) == (
        lax.broadcasted_iota(jnp.int32, (BAND, 128), 0)
    )

    def banded(t, row):
        return jnp.concatenate(
            [
                jnp.where(band_mask, jnp.broadcast_to(hrecv[t, j, row : row + 1, :], (BAND, 128)), 0.0)
                for j in range(PEERS)
            ],
            axis=0,
        )

    def build_onehots():
        source = lax.broadcasted_iota(jnp.int32, (128, 256), 0)
        target = lax.broadcasted_iota(jnp.int32, (128, 256), 1)
        expand = jnp.where(
            lax.shift_right_logical(source, 4) == lax.shift_right_logical(target, 6), 1.0, 0.0
        ).astype(BF16)
        position = lax.broadcasted_iota(jnp.int32, (1, 256), 1) & (SLOTS - 1)
        j = position & (PEERS - 1)
        dz, dy = offset(0, j & 3)
        for group in range(1, 4):
            group_z, group_y = offset(group, j & 3)
            inside = lax.shift_right_logical(j, 2) == group
            dz = jnp.where(inside, group_z, dz)
            dy = jnp.where(inside, group_y, dy)
        owner_z = (z + RING - dz) & (RING - 1)
        owner_y = (y + RING - dy) & (RING - 1)
        label = 4 * (owner_z * RING + owner_y) + lax.shift_right_logical(position, 4)
        label = label.astype(F32)
        weight = dot(banded(0, 22).astype(BF16), expand)
        for side in range(2):
            station = dot(banded(0, 20 + side).astype(BF16), expand)
            hit = station == label
            onehot = jnp.where(hit, 1.0, 0.0).astype(BF16)
            ohg[ROWS * side : ROWS * side + ROWS, 0:256] = onehot
            ohg[ROWS * side : ROWS * side + ROWS, 256:512] = onehot
            weighted = jnp.transpose(jnp.where(hit, weight, 0.0)).astype(BF16)
            ohs[:, 512 * side : 512 * side + 256] = weighted
            ohs[:, 512 * side + 256 : 512 * side + 512] = weighted

    def build_visibility(t):
        source = lax.broadcasted_iota(jnp.int32, (256, 256), 0) & 127
        target = lax.broadcasted_iota(jnp.int32, (256, 256), 1)
        expand = jnp.where(
            lax.shift_right_logical(source, 4) == lax.shift_right_logical(target, 5), 1.0, 0.0
        ).astype(BF16)
        for i in range(4):
            high, low = halves(banded(t, 16 + i))
            out = dot(jnp.concatenate([high, low], axis=1), expand)
            vis_x[2 * i] = out[:, 0:128]
            vis_x[2 * i + 1] = out[:, 128:256]

    def build_field(t):
        block = lane_block((PEERS, 128))
        for c in range(16):
            flat = jnp.concatenate([hrecv[t, j, c : c + 1, :] for j in range(PEERS)], axis=0)
            target = field if c < 8 else prior
            for s in range(4):
                target[c % 8, PEERS * s : PEERS * s + PEERS] = spread_lanes(
                    jnp.where(block == s, flat, 0.0)
                )

    def gather():
        block = lane_block((SLOTS, 128))
        for c in range(8):
            for at, part in enumerate(halves(field[c])):
                for q in range(QUARTERS):
                    first = 256 * at + SLOTS * q
                    jrhs[first : first + SLOTS, 128 * c : 128 * c + 128] = jnp.where(
                        block == q, part.astype(F32), 0.0
                    ).astype(BF16)
        for c in range(4):
            jpq[:, 256 * c : 256 * c + 256] = dot(ohg[...], jrhs[:, 256 * c : 256 * c + 256])

    def process(t, group):
        size = GROUP * BAND
        first = pl.multiple_of(group * size, size)
        rows = pl.ds(first, size)
        sources = pl.ds(group * GROUP, GROUP)
        coherent = [crecv[t, sources, c].reshape(size, 128) for c in range(8)]
        left = [jpq[rows, 128 * c : 128 * c + 128] for c in range(8)]
        right = [jpq[pl.ds(ROWS + first, size), 128 * c : 128 * c + 128] for c in range(8)]
        applied = product_adjoint(coherent, right)
        model = product(left, applied)
        outer = product(left, coherent)
        split = [jnp.concatenate(halves(x), axis=1) for x in model]
        total = dot(jnp.concatenate(split, axis=0), ones_blk[...])
        misfit = [vis_x[c, rows, :] - total[size * c : size * c + size] for c in range(8)]
        for side in range(2):
            if side == 0:
                out = product_adjoint(misfit, applied) + square_right(applied)
            else:
                out = adjoint_product(misfit, outer) + square_left(outer)
            for c in range(12):
                for at, part in enumerate(halves(out[c])):
                    terms[pl.ds(ROWS * (2 * side + at) + first, size), 128 * c : 128 * c + 128] = part

    def solve():
        block = lane_block((SLOTS, 128))
        sums = []
        for pair in range(6):
            res = dot(ohs[...], terms[:, 256 * pair : 256 * pair + 256])
            for half in range(2):
                part = res[:, 128 * half : 128 * half + 128]
                total = jnp.where(block == 0, part[0:SLOTS], 0.0)
                for q in range(1, QUARTERS):
                    total = jnp.where(block == q, part[SLOTS * q : SLOTS * q + SLOTS], total)
                sums.append(spread_lanes(total))
        current = [field[c] for c in range(8)]
        rhs = [sums[c] + prior[c] - PENALTY * current[c] for c in range(8)]
        top = sums[8] + PENALTY
        bottom = sums[9] + PENALTY
        real, imag = sums[10], sums[11]
        scale = DAMPING / (top * bottom - real * real - imag * imag)
        for i in range(2):
            a, b = rhs[2 * i], rhs[2 * i + 1]
            c, d = rhs[4 + 2 * i], rhs[4 + 2 * i + 1]
            field[2 * i] = current[2 * i] + scale * (a * bottom - b * real - d * imag)
            field[2 * i + 1] = current[2 * i + 1] + scale * (b * top - a * real + c * imag)
            field[4 + 2 * i] = current[4 + 2 * i] + scale * (c * bottom - d * real + b * imag)
            field[5 + 2 * i] = current[5 + 2 * i] + scale * (d * top - c * real - a * imag)

    def send_back(t):
        block = lane_block((PEERS, 128))
        for c in range(8):
            whole = field[c]
            flat = jnp.where(block == 0, whole[0:PEERS], 0.0)
            for s in range(1, 4):
                flat = jnp.where(block == s, whole[PEERS * s : PEERS * s + PEERS], flat)
            for j in range(PEERS):
                rsend[t, j, c : c + 1, :] = flat[j : j + 1]
        rrecv[t, me] = rsend[t, OWN]
        each_peer(lambda group, i: r_copy(t, group, i).start())

    def stage(t, _):
        own = own_copies(t)
        own[0].wait()
        each_peer(lambda group, i: h_copy(t, group, i).wait_recv())

        @pl.when(t == 0)
        def _():
            build_onehots()

        build_visibility(t)
        build_field(t)
        own[1].wait()

        def sweep(i, _):
            gather()

            def one_group(group, _):
                for source in range(4):
                    @pl.when((i == 0) & (group * 4 + source != OWN))
                    def _():
                        arrived(t, group * 4 + source).wait_recv()

                process(t, group)
                return 0

            lax.fori_loop(0, PEERS // GROUP, one_group, 0)
            solve()
            return 0

        lax.fori_loop(0, ITERS, sweep, 0)
        send_back(t)
        return 0

    lax.fori_loop(0, STAGES, stage, 0)

    def project(t, projected):
        each_peer(lambda group, i: r_copy(t, group, i).wait_recv())

        def one(d, projected):
            chan = PEERS * t + d
            blended = rrecv[t, d] + dual_t[chan] * (1.0 / PENALTY)
            return tuple(
                projected[m] + blended * (basis_at(basis, m, chan) * (1.0 / norm_of(m)))
                for m in range(NTERMS)
            )

        return lax.fori_loop(0, PEERS, one, projected)

    lane = lane_block((1, 128))

    def basis_rows(u, _):
        for m in range(NTERMS):
            row = jnp.full((1, 128), basis_at(basis, m, 4 * u), F32)
            for a in range(1, 4):
                row = jnp.where(lane == a, basis_at(basis, m, 4 * u + a), row)
            rows_out[m : m + 1, lanes_of(u)] = PENALTY * row
        return 0

    def finish(u, _):
        lanes = lanes_of(u)
        t, tile = u // 4, u % 4
        parts = swap_blocks([rrecv[t, 4 * tile + a] for a in range(4)])
        for s in range(4):
            jones_out[:, s, lanes] = parts[s]
            lifted_out[:, s, lanes] = dual[:, s, lanes] + PENALTY * parts[s]
        return 0

    def sent(t, _):
        for copy in (h_copy, c_copy):
            each_peer(lambda group, i, copy=copy: copy(t, group, i).wait_send())
        return 0

    projected = project(0, tuple(jnp.zeros((8, 128), F32) for _ in range(NTERMS)))
    lax.fori_loop(0, 8, basis_rows, 0)
    lax.fori_loop(0, 4, finish, 0)
    lax.fori_loop(0, STAGES, sent, 0)
    projected = project(1, projected)
    for m in range(NTERMS):
        psend[m] = projected[m]
        precv[fr, m] = projected[m]
    for g in (4, 5, 3, 6, 2, 7, 1):
        p_copy(g).start()
    lax.fori_loop(4, 8, finish, 0)
    for t in range(STAGES):
        each_peer(lambda group, i, t=t: r_copy(t, group, i).wait_send())
    for g in range(1, FREQS):
        p_copy(g).wait()
    block = lane_block((8, 128))
    for m in range(NTERMS):
        total = precv[0, m]
        for g in range(1, FREQS):
            total = total + precv[g, m]
        for s in range(4):
            smooth_out[m, :, s, :] = spread_lanes(jnp.where(block == s, total, 0.0))


def finish_kernel(jones, lifted, smooth, rows, jones_out, dual_hbm, cons_hbm, dual_out, cons_out, sem):
    copy = pltpu.make_async_copy(jones, jones_out, sem.at[0])
    copy.start()
    for m in range(NTERMS):
        cons_out[m] = smooth[m, :, :, 0:DIRS]
    cons_copy = pltpu.make_async_copy(cons_out, cons_hbm, sem.at[1])
    cons_copy.start()
    for tile in range(8):
        lanes = slice(128 * tile, 128 * tile + 128)
        scale = [jnp.broadcast_to(rows[m : m + 1, lanes], (4, 128)) for m in range(NTERMS)]
        for c in range(8):
            fitted = scale[0] * smooth[0, c]
            for m in range(1, NTERMS):
                fitted = fitted + scale[m] * smooth[m, c]
            dual_out[c, :, lanes] = lifted[c, :, lanes] - fitted
    dual_copy = pltpu.make_async_copy(dual_out, dual_hbm, sem.at[2])
    dual_copy.start()
    copy.wait()
    cons_copy.wait()
    dual_copy.wait()


def shards(coherency, visibility, span_lengths, station_pairs, jones_field, dual_field, consensus):
    vmem = pl.BlockSpec(memory_space=pltpu.VMEM)
    smem = pl.BlockSpec(memory_space=pltpu.SMEM)
    hbm = pl.BlockSpec(memory_space=pltpu.HBM)
    dma = pltpu.SemaphoreType.DMA
    basis = jnp.asarray(basis_table())
    operands = (
        coherency,
        jnp.transpose(visibility, (0, 2, 1)),
        span_lengths.reshape(1, -1),
        station_pairs,
        jones_field,
        dual_field,
        consensus,
    )
    jones, lifted, smooth, rows = pl.pallas_call(
        kernel,
        out_shape=(
            jax.ShapeDtypeStruct(jones_field.shape, F32),
            jax.ShapeDtypeStruct(dual_field.shape, F32),
            jax.ShapeDtypeStruct((NTERMS, 8, 4, 128), F32),
            jax.ShapeDtypeStruct((NTERMS, jones_field.shape[2]), F32),
        ),
        in_specs=[smem] + [hbm] * 7,
        out_specs=(vmem,) * 4,
        scratch_shapes=[pltpu.VMEM(x.shape, x.dtype) for x in operands]
        + [
            pltpu.VMEM((512, 512), BF16),
            pltpu.VMEM((STAGES, PEERS, 8, BAND, 128), F32),
            pltpu.VMEM((STAGES, PEERS, 8, BAND, 128), F32),
            pltpu.VMEM((STAGES, PEERS, HEAD, 128), F32),
            pltpu.VMEM((STAGES, PEERS, HEAD, 128), F32),
            pltpu.VMEM((STAGES, PEERS, 8, 128), F32),
            pltpu.VMEM((STAGES, PEERS, 8, 128), F32),
            pltpu.VMEM((NTERMS, 8, 128), F32),
            pltpu.VMEM((FREQS, NTERMS, 8, 128), F32),
            pltpu.VMEM((8, 128), F32),
            pltpu.VMEM((NTERMS, 8, 128), F32),
            pltpu.VMEM((STAGES * PEERS, 8, 128), F32),
            pltpu.VMEM((2 * ROWS, 8 * 128), F32),
            pltpu.VMEM((8, ROWS, 128), F32),
            pltpu.VMEM((4 * ROWS, 12 * 128), BF16),
            pltpu.VMEM((2 * ROWS, 512), BF16),
            pltpu.VMEM((QUARTERS * SLOTS, 4 * ROWS), BF16),
            pltpu.VMEM((2 * QUARTERS * SLOTS, 8 * 128), BF16),
            pltpu.VMEM((256, 128), BF16),
            pltpu.VMEM((8, SLOTS, 128), F32),
            pltpu.VMEM((8, SLOTS, 128), F32),
            dma((STAGES, PEERS)),
            dma((STAGES, PEERS)),
            dma((STAGES, PEERS)),
            dma((STAGES, PEERS)),
            dma((STAGES, PEERS)),
            dma((STAGES, PEERS)),
            dma((FREQS,)),
            dma((FREQS,)),
            dma((2 * STAGES,)),
            dma((7,)),
        ],
        compiler_params=pltpu.CompilerParams(
            collective_id=0, has_side_effects=True, vmem_limit_bytes=60 * 2**20
        ),
        name="calibrate",
    )(basis, *operands)
    return pl.pallas_call(
        finish_kernel,
        out_shape=(
            jax.ShapeDtypeStruct(jones_field.shape, F32),
            jax.ShapeDtypeStruct(dual_field.shape, F32),
            jax.ShapeDtypeStruct(consensus.shape, F32),
        ),
        in_specs=[vmem] * 4,
        out_specs=(hbm, hbm, hbm),
        scratch_shapes=[pltpu.VMEM(dual_field.shape, F32), pltpu.VMEM(consensus.shape, F32), dma((3,))],
        name="finish",
    )(jones, lifted, smooth, rows)


def solution(mesh):
    in_specs = (
        P(None, "bl", "freq"),
        P(None, "bl", "freq"),
        P("bl"),
        P(None, "bl"),
        P(None, "bl", "freq"),
        P(None, "bl", "freq"),
        P(None, None, "bl", None),
    )
    out_specs = (P(None, "bl", "freq"), P(None, "bl", "freq"), P(None, None, "bl", None))
    return jax.shard_map(shards, mesh=mesh, in_specs=in_specs, out_specs=out_specs, check_vma=False)
```

```python
import functools

import jax
import jax.numpy as jnp
import numpy as np
from jax import lax
from jax.experimental import pallas as pl
from jax.experimental.pallas import tpu as pltpu
from jax.sharding import PartitionSpec as P

CHANS = 256
ITERS = 2
NTERMS = 4
PENALTY = 4.0
DAMPING = 0.5

RING = 4
PEERS = 16
FREQS = 8
STAGES = 2
QUARTERS = 4
BAND = 16
DIRS = 32
SLOTS = 64
ROWS = PEERS * BAND
HEAD = 16
GROUP = 4
OWN = 4

MESH = pl.DeviceIdType.MESH
F32 = jnp.float32
BF16 = jnp.bfloat16


def basis_table():
    channel = np.arange(CHANS, dtype=np.float64) + 0.5
    order = np.arange(NTERMS, dtype=np.float64)
    return np.cos(np.pi * order[:, None] * channel[None, :] / CHANS).astype(np.float32)


def norm_of(term):
    return float(CHANS) if term == 0 else 0.5 * CHANS


def product(a, b):
    real, imag = [], []
    for i in range(2):
        for j in range(2):
            real.append(
                a[2 * i] * b[j]
                + a[2 * i + 1] * b[2 + j]
                - a[4 + 2 * i] * b[4 + j]
                - a[4 + 2 * i + 1] * b[4 + 2 + j]
            )
            imag.append(
                a[2 * i] * b[4 + j]
                + a[2 * i + 1] * b[4 + 2 + j]
                + a[4 + 2 * i] * b[j]
                + a[4 + 2 * i + 1] * b[2 + j]
            )
    return real + imag


def product_adjoint(a, b):
    real, imag = [], []
    for i in range(2):
        for j in range(2):
            real.append(
                a[2 * i] * b[2 * j]
                + a[2 * i + 1] * b[2 * j + 1]
                + a[4 + 2 * i] * b[4 + 2 * j]
                + a[4 + 2 * i + 1] * b[4 + 2 * j + 1]
            )
            imag.append(
                a[4 + 2 * i] * b[2 * j]
                + a[4 + 2 * i + 1] * b[2 * j + 1]
                - a[2 * i] * b[4 + 2 * j]
                - a[2 * i + 1] * b[4 + 2 * j + 1]
            )
    return real + imag


def adjoint_product(a, b):
    real, imag = [], []
    for i in range(2):
        for j in range(2):
            real.append(
                a[i] * b[j] + a[2 + i] * b[2 + j] + a[4 + i] * b[4 + j] + a[6 + i] * b[6 + j]
            )
            imag.append(
                a[i] * b[4 + j] + a[2 + i] * b[6 + j] - a[4 + i] * b[j] - a[6 + i] * b[2 + j]
            )
    return real + imag


def square_right(a):
    top = a[0] * a[0] + a[1] * a[1] + a[4] * a[4] + a[5] * a[5]
    bottom = a[2] * a[2] + a[3] * a[3] + a[6] * a[6] + a[7] * a[7]
    real = a[0] * a[2] + a[4] * a[6] + a[1] * a[3] + a[5] * a[7]
    imag = a[4] * a[2] - a[0] * a[6] + a[5] * a[3] - a[1] * a[7]
    return [top, bottom, real, imag]


def square_left(a):
    return square_right([a[0], a[2], a[1], a[3], -a[4], -a[6], -a[5], -a[7]])


def halves(x):
    high = x.astype(BF16)
    return high, (x - high.astype(F32)).astype(BF16)


def lane_block(shape):
    return lax.shift_right_logical(lax.broadcasted_iota(jnp.int32, shape, len(shape) - 1), 5)


def swap_blocks(x):
    block = lane_block(x[0].shape)
    left = block < 2
    even = (block & 1) == 0
    halfway = [None] * 4
    for low in range(2):
        first, second = x[low], x[2 + low]
        halfway[low] = jnp.where(left, first, pltpu.roll(second, 64, 1))
        halfway[2 + low] = jnp.where(left, pltpu.roll(first, 64, 1), second)
    out = [None] * 4
    for high in range(2):
        first, second = halfway[2 * high], halfway[2 * high + 1]
        out[2 * high] = jnp.where(even, first, pltpu.roll(second, 32, 1))
        out[2 * high + 1] = jnp.where(even, pltpu.roll(first, 96, 1), second)
    return out


def spread_lanes(x):
    x = x + pltpu.roll(x, 64, 1)
    return x + pltpu.roll(x, 32, 1)


def dot(a, b):
    return jnp.dot(a, b, preferred_element_type=F32)


def basis_at(basis, term, chan):
    return basis[term, lax.axis_index("freq") * (CHANS // FREQS) + chan]


def offset(group, i):
    low, high = i % 2, i // 2
    sign = 1 + 2 * high
    if group == 0:
        return 2 * (1 - low) + sign * low, sign * (1 - low) + 2 * low
    if group == 1:
        return 2 * low, 2 * ((low + high) % 2)
    if group == 2:
        return 1 + 2 * low, 1 + 2 * ((low + high) % 2)
    return low * sign, (1 - low) * sign


def kernel(
    basis, coh_hbm, vis_hbm, span_hbm, pairs_hbm, jones_hbm, dual_hbm, cons_hbm,
    jones_out, lifted_out, smooth_out, rows_out,
    coh, vis, span, pairs, jones, dual, cons,
    perm, csend, crecv, hsend, hrecv, rsend, rrecv, psend, precv,
    meta, const, dual_t, jpq, vis_x, terms, ohg, ohs, jrhs, ones_blk, field, prior,
    csend_sem, crecv_sem, hsend_sem, hrecv_sem, rsend_sem, rrecv_sem, psend_sem, precv_sem, own_sem, in_sem, qsend_sem, qrecv_sem,
):
    me = lax.axis_index("bl")
    fr = lax.axis_index("freq")
    z, y = me // RING, me % RING

    def ahead(group, i):
        dz, dy = offset(group, i)
        return lax.rem(z + dz, RING) * RING + lax.rem(y + dy, RING)

    def behind(group, i):
        dz, dy = offset(group, i)
        return lax.rem(z + RING - dz, RING) * RING + lax.rem(y + RING - dy, RING)

    def each_peer(step):
        for group in range(4):
            def one(i, _, group=group):
                step(group, i)
                return 0

            lax.fori_loop(1 if group == OWN // GROUP else 0, 4, one, 0)

    def freq_ahead(g):
        return lax.rem(fr + g, FREQS)


    loads = [
        pltpu.make_async_copy(source, target, in_sem.at[i])
        for i, (source, target) in enumerate(
            [
                (jones_hbm, jones), (dual_hbm, dual), (cons_hbm, cons), (vis_hbm, vis),
                (span_hbm, span), (pairs_hbm, pairs), (coh_hbm, coh),
            ]
        )
    ]
    for load in loads:
        load.start()

    barrier = pltpu.get_barrier_semaphore()
    each_peer(
        lambda group, i: pl.semaphore_signal(
            barrier, inc=1, device_id={"bl": ahead(group, i)}, device_id_type=MESH
        )
    )
    for g in range(1, FREQS):
        pl.semaphore_signal(barrier, inc=1, device_id={"freq": freq_ahead(g)}, device_id_type=MESH)

    def c_copy(t, group, i):
        j = 4 * group + i
        return pltpu.make_async_remote_copy(
            src_ref=csend.at[t, ahead(group, i)], dst_ref=crecv.at[t, j],
            send_sem=csend_sem.at[t, j], recv_sem=crecv_sem.at[t, j],
            device_id={"bl": ahead(group, i)}, device_id_type=MESH,
        )

    def h_copy(t, group, i):
        j = 4 * group + i
        return pltpu.make_async_remote_copy(
            src_ref=hsend.at[t, ahead(group, i), pl.ds(0, HEAD)], dst_ref=hrecv.at[t, j, pl.ds(0, HEAD)],
            send_sem=hsend_sem.at[t, j], recv_sem=hrecv_sem.at[t, j],
            device_id={"bl": ahead(group, i)}, device_id_type=MESH,
        )

    def q_copy(t, group, i):
        j = 4 * group + i
        return pltpu.make_async_remote_copy(
            src_ref=hsend.at[t, ahead(group, i), pl.ds(HEAD, 8)], dst_ref=hrecv.at[t, j, pl.ds(HEAD, 8)],
            send_sem=qsend_sem.at[t, j], recv_sem=qrecv_sem.at[t, j],
            device_id={"bl": ahead(group, i)}, device_id_type=MESH,
        )

    def r_copy(t, group, i):
        j = 4 * group + i
        return pltpu.make_async_remote_copy(
            src_ref=rsend.at[t, j], dst_ref=rrecv.at[t, me],
            send_sem=rsend_sem.at[t, j], recv_sem=rrecv_sem.at[t, j],
            device_id={"bl": behind(group, i)}, device_id_type=MESH,
        )

    def arrived(t, j):
        return pltpu.make_async_remote_copy(
            src_ref=csend.at[t, j], dst_ref=crecv.at[t, j],
            send_sem=csend_sem.at[t, j], recv_sem=crecv_sem.at[t, j],
            device_id={"bl": ahead(3, 0)}, device_id_type=MESH,
        )

    def p_copy(g):
        return pltpu.make_async_remote_copy(
            src_ref=psend, dst_ref=precv.at[fr],
            send_sem=psend_sem.at[g], recv_sem=precv_sem.at[g],
            device_id={"freq": freq_ahead(g)}, device_id_type=MESH,
        )

    def own_copies(t):
        return (
            pltpu.make_async_copy(hsend.at[t, me], hrecv.at[t, OWN], own_sem.at[2 * t]),
            pltpu.make_async_copy(csend.at[t, me], crecv.at[t, OWN], own_sem.at[2 * t + 1]),
        )


    def lanes_of(u):
        return pl.ds(pl.multiple_of(128 * u, 128), 128)

    def build_head(u, _):
        t, tile = u // 4, u % 4
        lanes = lanes_of(u)
        j_tile = swap_blocks([jones[:, s, lanes] for s in range(4)])
        d_tile = swap_blocks([dual[:, s, lanes] for s in range(4)])
        for a in range(4):
            d = 4 * tile + a
            chan = 4 * u + a
            smooth = const[0] * basis_at(basis, 0, chan)
            for m in range(1, NTERMS):
                smooth = smooth + const[m] * basis_at(basis, m, chan)
            dual_t[chan] = d_tile[a]
            hsend[t, d, 0:8, :] = j_tile[a]
            hsend[t, d, 16:24, :] = PENALTY * smooth - d_tile[a]
        return 0

    def build_c(u, _):
        t, tile = u // 4, u % 4
        lanes = lanes_of(u)
        rows = jnp.concatenate(
            [coh[:, BAND * q : BAND * q + BAND, lanes].reshape(8 * BAND, 128) for q in range(QUARTERS)],
            axis=1,
        )
        out = dot(rows, perm[...])
        for a in range(4):
            csend[t, 4 * tile + a] = out[:, 128 * a : 128 * a + 128].reshape(8, BAND, 128)
        return 0

    at_row = lax.broadcasted_iota(jnp.int32, (128, 128), 0)
    apart = at_row - lax.broadcasted_iota(jnp.int32, (128, 128), 1)
    for a in range(4):
        for q in range(QUARTERS):
            hit = (apart == DIRS * (a - q)) & (lax.shift_right_logical(at_row, 5) == a)
            perm[128 * q : 128 * q + 128, 128 * a : 128 * a + 128] = jnp.where(hit, 1.0, 0.0).astype(BF16)

    for load in loads[:6]:
        load.wait()
    for m in range(NTERMS):
        for s in range(4):
            const[m, :, DIRS * s : DIRS * s + DIRS] = cons[m, :, s, :]
    meta[...] = jnp.zeros_like(meta)
    meta[0:2, 0:64] = pairs[...].astype(F32)
    meta[2:3, 0:64] = span[...].astype(F32)
    for t in range(STAGES):
        for i in range(4):
            pair = [vis[2 * i + half, PEERS * t : PEERS * t + PEERS, :] for half in range(2)]
            hsend[t, :, 8 + i, :] = jnp.concatenate(pair, axis=1)
        for d in range(PEERS):
            hsend[t, d, 12:16, :] = meta[0:4, :]
    lax.fori_loop(0, 8, build_head, 0)
    for load in loads[6:]:
        load.wait()
    lax.fori_loop(0, 4, build_c, 0)
    pl.semaphore_wait(barrier, PEERS - 1 + FREQS - 1)

    def send(t, _):
        for copy in own_copies(t):
            copy.start()
        each_peer(lambda group, i: h_copy(t, group, i).start())
        each_peer(lambda group, i: c_copy(t, group, i).start())
        each_peer(lambda group, i: q_copy(t, group, i).start())

        @pl.when(t == 0)
        def _():
            lax.fori_loop(4, 8, build_c, 0)

        return 0

    lax.fori_loop(0, STAGES, send, 0)

    row_block = lax.shift_right_logical(lax.broadcasted_iota(jnp.int32, (256, 128), 0), 5) & 3
    ones_blk[...] = jnp.where(row_block == lane_block((256, 128)), 1.0, 0.0).astype(BF16)

    band_mask = (lax.broadcasted_iota(jnp.int32, (BAND, 128), 1) & (BAND - 1)) == (
        lax.broadcasted_iota(jnp.int32, (BAND, 128), 0)
    )

    def banded(t, row):
        return jnp.concatenate(
            [
                jnp.where(band_mask, jnp.broadcast_to(hrecv[t, j, row : row + 1, :], (BAND, 128)), 0.0)
                for j in range(PEERS)
            ],
            axis=0,
        )

    def build_onehots():
        source = lax.broadcasted_iota(jnp.int32, (128, 256), 0)
        target = lax.broadcasted_iota(jnp.int32, (128, 256), 1)
        expand = jnp.where(
            lax.shift_right_logical(source, 4) == lax.shift_right_logical(target, 6), 1.0, 0.0
        ).astype(BF16)
        position = lax.broadcasted_iota(jnp.int32, (1, 256), 1) & (SLOTS - 1)
        j = position & (PEERS - 1)
        dz, dy = offset(0, j & 3)
        for group in range(1, 4):
            group_z, group_y = offset(group, j & 3)
            inside = lax.shift_right_logical(j, 2) == group
            dz = jnp.where(inside, group_z, dz)
            dy = jnp.where(inside, group_y, dy)
        owner_z = (z + RING - dz) & (RING - 1)
        owner_y = (y + RING - dy) & (RING - 1)
        label = 4 * (owner_z * RING + owner_y) + lax.shift_right_logical(position, 4)
        label = label.astype(F32)
        weight = dot(banded(0, 14).astype(BF16), expand)
        for side in range(2):
            station = dot(banded(0, 12 + side).astype(BF16), expand)
            hit = station == label
            onehot = jnp.where(hit, 1.0, 0.0).astype(BF16)
            ohg[ROWS * side : ROWS * side + ROWS, 0:256] = onehot
            ohg[ROWS * side : ROWS * side + ROWS, 256:512] = onehot
            weighted = jnp.transpose(jnp.where(hit, weight, 0.0)).astype(BF16)
            ohs[:, 512 * side : 512 * side + 256] = weighted
            ohs[:, 512 * side + 256 : 512 * side + 512] = weighted

    def build_visibility(t):
        source = lax.broadcasted_iota(jnp.int32, (256, 256), 0) & 127
        target = lax.broadcasted_iota(jnp.int32, (256, 256), 1)
        expand = jnp.where(
            lax.shift_right_logical(source, 4) == lax.shift_right_logical(target, 5), 1.0, 0.0
        ).astype(BF16)
        for i in range(4):
            high, low = halves(banded(t, 8 + i))
            out = dot(jnp.concatenate([high, low], axis=1), expand)
            vis_x[2 * i] = out[:, 0:128]
            vis_x[2 * i + 1] = out[:, 128:256]

    def unpack(t, first, target):
        block = lane_block((PEERS, 128))
        for c in range(8):
            flat = jnp.concatenate(
                [hrecv[t, j, first + c : first + c + 1, :] for j in range(PEERS)], axis=0
            )
            for s in range(4):
                target[c, PEERS * s : PEERS * s + PEERS] = spread_lanes(
                    jnp.where(block == s, flat, 0.0)
                )

    def gather():
        block = lane_block((SLOTS, 128))
        for c in range(8):
            for at, part in enumerate(halves(field[c])):
                for q in range(QUARTERS):
                    first = 256 * at + SLOTS * q
                    jrhs[first : first + SLOTS, 128 * c : 128 * c + 128] = jnp.where(
                        block == q, part.astype(F32), 0.0
                    ).astype(BF16)
        for c in range(4):
            jpq[:, 256 * c : 256 * c + 256] = dot(ohg[...], jrhs[:, 256 * c : 256 * c + 256])

    def process(t, group):
        size = GROUP * BAND
        first = pl.multiple_of(group * size, size)
        rows = pl.ds(first, size)
        sources = pl.ds(group * GROUP, GROUP)
        coherent = [crecv[t, sources, c].reshape(size, 128) for c in range(8)]
        left = [jpq[rows, 128 * c : 128 * c + 128] for c in range(8)]
        right = [jpq[pl.ds(ROWS + first, size), 128 * c : 128 * c + 128] for c in range(8)]
        applied = product_adjoint(coherent, right)
        model = product(left, applied)
        outer = product(left, coherent)
        split = [jnp.concatenate(halves(x), axis=1) for x in model]
        total = dot(jnp.concatenate(split, axis=0), ones_blk[...])
        misfit = [vis_x[c, rows, :] - total[size * c : size * c + size] for c in range(8)]
        for side in range(2):
            if side == 0:
                out = product_adjoint(misfit, applied) + square_right(applied)
            else:
                out = adjoint_product(misfit, outer) + square_left(outer)
            for c in range(12):
                for at, part in enumerate(halves(out[c])):
                    terms[pl.ds(ROWS * (2 * side + at) + first, size), 128 * c : 128 * c + 128] = part

    def solve():
        block = lane_block((SLOTS, 128))
        sums = []
        for pair in range(6):
            res = dot(ohs[...], terms[:, 256 * pair : 256 * pair + 256])
            for half in range(2):
                part = res[:, 128 * half : 128 * half + 128]
                total = jnp.where(block == 0, part[0:SLOTS], 0.0)
                for q in range(1, QUARTERS):
                    total = jnp.where(block == q, part[SLOTS * q : SLOTS * q + SLOTS], total)
                sums.append(spread_lanes(total))
        current = [field[c] for c in range(8)]
        rhs = [sums[c] + prior[c] - PENALTY * current[c] for c in range(8)]
        top = sums[8] + PENALTY
        bottom = sums[9] + PENALTY
        real, imag = sums[10], sums[11]
        scale = DAMPING / (top * bottom - real * real - imag * imag)
        for i in range(2):
            a, b = rhs[2 * i], rhs[2 * i + 1]
            c, d = rhs[4 + 2 * i], rhs[4 + 2 * i + 1]
            field[2 * i] = current[2 * i] + scale * (a * bottom - b * real - d * imag)
            field[2 * i + 1] = current[2 * i + 1] + scale * (b * top - a * real + c * imag)
            field[4 + 2 * i] = current[4 + 2 * i] + scale * (c * bottom - d * real + b * imag)
            field[5 + 2 * i] = current[5 + 2 * i] + scale * (d * top - c * real - a * imag)

    def send_back(t):
        block = lane_block((PEERS, 128))
        for c in range(8):
            whole = field[c]
            flat = jnp.where(block == 0, whole[0:PEERS], 0.0)
            for s in range(1, 4):
                flat = jnp.where(block == s, whole[PEERS * s : PEERS * s + PEERS], flat)
            for j in range(PEERS):
                rsend[t, j, c : c + 1, :] = flat[j : j + 1]
        rrecv[t, me] = rsend[t, OWN]
        each_peer(lambda group, i: r_copy(t, group, i).start())

    def stage(t, _):
        own = own_copies(t)
        own[0].wait()
        each_peer(lambda group, i: h_copy(t, group, i).wait_recv())

        @pl.when(t == 0)
        def _():
            build_onehots()

        build_visibility(t)
        unpack(t, 0, field)
        own[1].wait()

        def sweep(i, _):
            gather()

            def one_group(group, _):
                for source in range(4):
                    @pl.when((i == 0) & (group * 4 + source != OWN))
                    def _():
                        arrived(t, group * 4 + source).wait_recv()

                process(t, group)
                return 0

            lax.fori_loop(0, PEERS // GROUP, one_group, 0)
            @pl.when(i == 0)
            def _():
                each_peer(lambda group, i: q_copy(t, group, i).wait_recv())
                unpack(t, HEAD, prior)

            solve()
            return 0

        lax.fori_loop(0, ITERS, sweep, 0)
        send_back(t)
        return 0

    lax.fori_loop(0, STAGES, stage, 0)

    def project(t, projected):
        each_peer(lambda group, i: r_copy(t, group, i).wait_recv())

        def one(d, projected):
            chan = PEERS * t + d
            blended = rrecv[t, d] + dual_t[chan] * (1.0 / PENALTY)
            return tuple(
                projected[m] + blended * (basis_at(basis, m, chan) * (1.0 / norm_of(m)))
                for m in range(NTERMS)
            )

        return lax.fori_loop(0, PEERS, one, projected)

    lane = lane_block((1, 128))

    def basis_rows(u, _):
        for m in range(NTERMS):
            row = jnp.full((1, 128), basis_at(basis, m, 4 * u), F32)
            for a in range(1, 4):
                row = jnp.where(lane == a, basis_at(basis, m, 4 * u + a), row)
            rows_out[m : m + 1, lanes_of(u)] = PENALTY * row
        return 0

    def finish(u, _):
        lanes = lanes_of(u)
        t, tile = u // 4, u % 4
        parts = swap_blocks([rrecv[t, 4 * tile + a] for a in range(4)])
        for s in range(4):
            jones_out[:, s, lanes] = parts[s]
            lifted_out[:, s, lanes] = dual[:, s, lanes] + PENALTY * parts[s]
        return 0

    def sent(t, _):
        for copy in (h_copy, q_copy, c_copy):
            each_peer(lambda group, i, copy=copy: copy(t, group, i).wait_send())
        return 0

    projected = project(0, tuple(jnp.zeros((8, 128), F32) for _ in range(NTERMS)))
    lax.fori_loop(0, 8, basis_rows, 0)
    lax.fori_loop(0, 4, finish, 0)
    lax.fori_loop(0, STAGES, sent, 0)
    projected = project(1, projected)
    for m in range(NTERMS):
        psend[m] = projected[m]
        precv[fr, m] = projected[m]
    for g in (4, 5, 3, 6, 2, 7, 1):
        p_copy(g).start()
    lax.fori_loop(4, 8, finish, 0)
    for t in range(STAGES):
        each_peer(lambda group, i, t=t: r_copy(t, group, i).wait_send())
    for g in range(1, FREQS):
        p_copy(g).wait()
    block = lane_block((8, 128))
    for m in range(NTERMS):
        total = precv[0, m]
        for g in range(1, FREQS):
            total = total + precv[g, m]
        for s in range(4):
            smooth_out[m, :, s, :] = spread_lanes(jnp.where(block == s, total, 0.0))


def finish_kernel(jones, lifted, smooth, rows, jones_out, dual_hbm, cons_hbm, dual_out, cons_out, sem):
    copy = pltpu.make_async_copy(jones, jones_out, sem.at[0])
    copy.start()
    for m in range(NTERMS):
        cons_out[m] = smooth[m, :, :, 0:DIRS]
    cons_copy = pltpu.make_async_copy(cons_out, cons_hbm, sem.at[1])
    cons_copy.start()
    for tile in range(8):
        lanes = slice(128 * tile, 128 * tile + 128)
        scale = [jnp.broadcast_to(rows[m : m + 1, lanes], (4, 128)) for m in range(NTERMS)]
        for c in range(8):
            fitted = scale[0] * smooth[0, c]
            for m in range(1, NTERMS):
                fitted = fitted + scale[m] * smooth[m, c]
            dual_out[c, :, lanes] = lifted[c, :, lanes] - fitted
    dual_copy = pltpu.make_async_copy(dual_out, dual_hbm, sem.at[2])
    dual_copy.start()
    copy.wait()
    cons_copy.wait()
    dual_copy.wait()


def shards(coherency, visibility, span_lengths, station_pairs, jones_field, dual_field, consensus):
    vmem = pl.BlockSpec(memory_space=pltpu.VMEM)
    smem = pl.BlockSpec(memory_space=pltpu.SMEM)
    hbm = pl.BlockSpec(memory_space=pltpu.HBM)
    dma = pltpu.SemaphoreType.DMA
    basis = jnp.asarray(basis_table())
    operands = (
        coherency,
        jnp.transpose(visibility, (0, 2, 1)),
        span_lengths.reshape(1, -1),
        station_pairs,
        jones_field,
        dual_field,
        consensus,
    )
    jones, lifted, smooth, rows = pl.pallas_call(
        kernel,
        out_shape=(
            jax.ShapeDtypeStruct(jones_field.shape, F32),
            jax.ShapeDtypeStruct(dual_field.shape, F32),
            jax.ShapeDtypeStruct((NTERMS, 8, 4, 128), F32),
            jax.ShapeDtypeStruct((NTERMS, jones_field.shape[2]), F32),
        ),
        in_specs=[smem] + [hbm] * 7,
        out_specs=(vmem,) * 4,
        scratch_shapes=[pltpu.VMEM(x.shape, x.dtype) for x in operands]
        + [
            pltpu.VMEM((512, 512), BF16),
            pltpu.VMEM((STAGES, PEERS, 8, BAND, 128), F32),
            pltpu.VMEM((STAGES, PEERS, 8, BAND, 128), F32),
            pltpu.VMEM((STAGES, PEERS, HEAD + 8, 128), F32),
            pltpu.VMEM((STAGES, PEERS, HEAD + 8, 128), F32),
            pltpu.VMEM((STAGES, PEERS, 8, 128), F32),
            pltpu.VMEM((STAGES, PEERS, 8, 128), F32),
            pltpu.VMEM((NTERMS, 8, 128), F32),
            pltpu.VMEM((FREQS, NTERMS, 8, 128), F32),
            pltpu.VMEM((8, 128), F32),
            pltpu.VMEM((NTERMS, 8, 128), F32),
            pltpu.VMEM((STAGES * PEERS, 8, 128), F32),
            pltpu.VMEM((2 * ROWS, 8 * 128), F32),
            pltpu.VMEM((8, ROWS, 128), F32),
            pltpu.VMEM((4 * ROWS, 12 * 128), BF16),
            pltpu.VMEM((2 * ROWS, 512), BF16),
            pltpu.VMEM((QUARTERS * SLOTS, 4 * ROWS), BF16),
            pltpu.VMEM((2 * QUARTERS * SLOTS, 8 * 128), BF16),
            pltpu.VMEM((256, 128), BF16),
            pltpu.VMEM((8, SLOTS, 128), F32),
            pltpu.VMEM((8, SLOTS, 128), F32),
            dma((STAGES, PEERS)),
            dma((STAGES, PEERS)),
            dma((STAGES, PEERS)),
            dma((STAGES, PEERS)),
            dma((STAGES, PEERS)),
            dma((STAGES, PEERS)),
            dma((FREQS,)),
            dma((FREQS,)),
            dma((2 * STAGES,)),
            dma((7,)),
            dma((STAGES, PEERS)),
            dma((STAGES, PEERS)),
        ],
        compiler_params=pltpu.CompilerParams(
            collective_id=0, has_side_effects=True, vmem_limit_bytes=60 * 2**20
        ),
        name="calibrate",
    )(basis, *operands)
    return pl.pallas_call(
        finish_kernel,
        out_shape=(
            jax.ShapeDtypeStruct(jones_field.shape, F32),
            jax.ShapeDtypeStruct(dual_field.shape, F32),
            jax.ShapeDtypeStruct(consensus.shape, F32),
        ),
        in_specs=[vmem] * 4,
        out_specs=(hbm, hbm, hbm),
        scratch_shapes=[pltpu.VMEM(dual_field.shape, F32), pltpu.VMEM(consensus.shape, F32), dma((3,))],
        name="finish",
    )(jones, lifted, smooth, rows)


def solution(mesh):
    in_specs = (
        P(None, "bl", "freq"),
        P(None, "bl", "freq"),
        P("bl"),
        P(None, "bl"),
        P(None, "bl", "freq"),
        P(None, "bl", "freq"),
        P(None, None, "bl", None),
    )
    out_specs = (P(None, "bl", "freq"), P(None, "bl", "freq"), P(None, None, "bl", None))
    return jax.shard_map(shards, mesh=mesh, in_specs=in_specs, out_specs=out_specs, check_vma=False)
```

```python
import functools

import jax
import jax.numpy as jnp
import numpy as np
from jax import lax
from jax.experimental import pallas as pl
from jax.experimental.pallas import tpu as pltpu
from jax.sharding import PartitionSpec as P

CHANS = 256
ITERS = 2
NTERMS = 4
PENALTY = 4.0
DAMPING = 0.5

RING = 4
PEERS = 16
FREQS = 8
STAGES = 2
QUARTERS = 4
BAND = 16
DIRS = 32
SLOTS = 64
ROWS = PEERS * BAND
HEAD = 16
GROUP = 4
OWN = 4

MESH = pl.DeviceIdType.MESH
F32 = jnp.float32
BF16 = jnp.bfloat16


def basis_table():
    channel = np.arange(CHANS, dtype=np.float64) + 0.5
    order = np.arange(NTERMS, dtype=np.float64)
    return np.cos(np.pi * order[:, None] * channel[None, :] / CHANS).astype(np.float32)


def norm_of(term):
    return float(CHANS) if term == 0 else 0.5 * CHANS


def product(a, b):
    real, imag = [], []
    for i in range(2):
        for j in range(2):
            real.append(
                a[2 * i] * b[j]
                + a[2 * i + 1] * b[2 + j]
                - a[4 + 2 * i] * b[4 + j]
                - a[4 + 2 * i + 1] * b[4 + 2 + j]
            )
            imag.append(
                a[2 * i] * b[4 + j]
                + a[2 * i + 1] * b[4 + 2 + j]
                + a[4 + 2 * i] * b[j]
                + a[4 + 2 * i + 1] * b[2 + j]
            )
    return real + imag


def product_adjoint(a, b):
    real, imag = [], []
    for i in range(2):
        for j in range(2):
            real.append(
                a[2 * i] * b[2 * j]
                + a[2 * i + 1] * b[2 * j + 1]
                + a[4 + 2 * i] * b[4 + 2 * j]
                + a[4 + 2 * i + 1] * b[4 + 2 * j + 1]
            )
            imag.append(
                a[4 + 2 * i] * b[2 * j]
                + a[4 + 2 * i + 1] * b[2 * j + 1]
                - a[2 * i] * b[4 + 2 * j]
                - a[2 * i + 1] * b[4 + 2 * j + 1]
            )
    return real + imag


def adjoint_product(a, b):
    real, imag = [], []
    for i in range(2):
        for j in range(2):
            real.append(
                a[i] * b[j] + a[2 + i] * b[2 + j] + a[4 + i] * b[4 + j] + a[6 + i] * b[6 + j]
            )
            imag.append(
                a[i] * b[4 + j] + a[2 + i] * b[6 + j] - a[4 + i] * b[j] - a[6 + i] * b[2 + j]
            )
    return real + imag


def square_right(a):
    top = a[0] * a[0] + a[1] * a[1] + a[4] * a[4] + a[5] * a[5]
    bottom = a[2] * a[2] + a[3] * a[3] + a[6] * a[6] + a[7] * a[7]
    real = a[0] * a[2] + a[4] * a[6] + a[1] * a[3] + a[5] * a[7]
    imag = a[4] * a[2] - a[0] * a[6] + a[5] * a[3] - a[1] * a[7]
    return [top, bottom, real, imag]


def square_left(a):
    return square_right([a[0], a[2], a[1], a[3], -a[4], -a[6], -a[5], -a[7]])


def halves(x):
    high = x.astype(BF16)
    return high, (x - high.astype(F32)).astype(BF16)


def lane_block(shape):
    return lax.shift_right_logical(lax.broadcasted_iota(jnp.int32, shape, len(shape) - 1), 5)


def swap_blocks(x):
    block = lane_block(x[0].shape)
    left = block < 2
    even = (block & 1) == 0
    halfway = [None] * 4
    for low in range(2):
        first, second = x[low], x[2 + low]
        halfway[low] = jnp.where(left, first, pltpu.roll(second, 64, 1))
        halfway[2 + low] = jnp.where(left, pltpu.roll(first, 64, 1), second)
    out = [None] * 4
    for high in range(2):
        first, second = halfway[2 * high], halfway[2 * high + 1]
        out[2 * high] = jnp.where(even, first, pltpu.roll(second, 32, 1))
        out[2 * high + 1] = jnp.where(even, pltpu.roll(first, 96, 1), second)
    return out


def spread_lanes(x):
    x = x + pltpu.roll(x, 64, 1)
    return x + pltpu.roll(x, 32, 1)


def dot(a, b):
    return jnp.dot(a, b, preferred_element_type=F32)


def basis_at(basis, term, chan):
    return basis[term, lax.axis_index("freq") * (CHANS // FREQS) + chan]


def offset(group, i):
    low, high = i % 2, i // 2
    sign = 1 + 2 * high
    if group == 0:
        return 2 * (1 - low) + sign * low, sign * (1 - low) + 2 * low
    if group == 1:
        return 2 * low, 2 * ((low + high) % 2)
    if group == 2:
        return 1 + 2 * low, 1 + 2 * ((low + high) % 2)
    return low * sign, (1 - low) * sign


def kernel(
    basis, coh_hbm, vis_hbm, span_hbm, pairs_hbm, jones_hbm, dual_hbm, cons_hbm,
    jones_out, lifted_out, smooth_out, rows_out,
    coh, vis, span, pairs, jones, dual, cons,
    perm, csend, crecv, hsend, hrecv, rsend, rrecv, psend, precv,
    meta, const, dual_t, jpq, vis_x, terms, ohg, ohs, jrhs, ones_blk, field, prior,
    csend_sem, crecv_sem, hsend_sem, hrecv_sem, rsend_sem, rrecv_sem, psend_sem, precv_sem, own_sem, in_sem, qsend_sem, qrecv_sem,
):
    me = lax.axis_index("bl")
    fr = lax.axis_index("freq")
    z, y = me // RING, me % RING

    def ahead(group, i):
        dz, dy = offset(group, i)
        return lax.rem(z + dz, RING) * RING + lax.rem(y + dy, RING)

    def behind(group, i):
        dz, dy = offset(group, i)
        return lax.rem(z + RING - dz, RING) * RING + lax.rem(y + RING - dy, RING)

    def each_peer(step):
        for group in range(4):
            def one(i, _, group=group):
                step(group, i)
                return 0

            lax.fori_loop(1 if group == OWN // GROUP else 0, 4, one, 0)

    def freq_ahead(g):
        return lax.rem(fr + g, FREQS)


    loads = [
        pltpu.make_async_copy(source, target, in_sem.at[i])
        for i, (source, target) in enumerate(
            [
                (jones_hbm, jones), (dual_hbm, dual), (cons_hbm, cons), (vis_hbm, vis),
                (span_hbm, span), (pairs_hbm, pairs), (coh_hbm, coh),
            ]
        )
    ]
    for load in loads:
        load.start()

    barrier = pltpu.get_barrier_semaphore()
    each_peer(
        lambda group, i: pl.semaphore_signal(
            barrier, inc=1, device_id={"bl": ahead(group, i)}, device_id_type=MESH
        )
    )
    for g in range(1, FREQS):
        pl.semaphore_signal(barrier, inc=1, device_id={"freq": freq_ahead(g)}, device_id_type=MESH)

    def c_copy(t, group, i):
        j = 4 * group + i
        return pltpu.make_async_remote_copy(
            src_ref=csend.at[t, ahead(group, i)], dst_ref=crecv.at[t, j],
            send_sem=csend_sem.at[t, j], recv_sem=crecv_sem.at[t, j],
            device_id={"bl": ahead(group, i)}, device_id_type=MESH,
        )

    def h_copy(t, group, i):
        j = 4 * group + i
        return pltpu.make_async_remote_copy(
            src_ref=hsend.at[t, ahead(group, i), pl.ds(0, HEAD)], dst_ref=hrecv.at[t, j, pl.ds(0, HEAD)],
            send_sem=hsend_sem.at[t, j], recv_sem=hrecv_sem.at[t, j],
            device_id={"bl": ahead(group, i)}, device_id_type=MESH,
        )

    def q_copy(t, group, i):
        j = 4 * group + i
        return pltpu.make_async_remote_copy(
            src_ref=hsend.at[t, ahead(group, i), pl.ds(HEAD, 8)], dst_ref=hrecv.at[t, j, pl.ds(HEAD, 8)],
            send_sem=qsend_sem.at[t, j], recv_sem=qrecv_sem.at[t, j],
            device_id={"bl": ahead(group, i)}, device_id_type=MESH,
        )

    def r_copy(t, group, i):
        j = 4 * group + i
        return pltpu.make_async_remote_copy(
            src_ref=rsend.at[t, j], dst_ref=rrecv.at[t, me],
            send_sem=rsend_sem.at[t, j], recv_sem=rrecv_sem.at[t, j],
            device_id={"bl": behind(group, i)}, device_id_type=MESH,
        )

    def arrived(t, j):
        return pltpu.make_async_remote_copy(
            src_ref=csend.at[t, j], dst_ref=crecv.at[t, j],
            send_sem=csend_sem.at[t, j], recv_sem=crecv_sem.at[t, j],
            device_id={"bl": ahead(3, 0)}, device_id_type=MESH,
        )

    def p_copy(g):
        return pltpu.make_async_remote_copy(
            src_ref=psend, dst_ref=precv.at[fr],
            send_sem=psend_sem.at[g], recv_sem=precv_sem.at[g],
            device_id={"freq": freq_ahead(g)}, device_id_type=MESH,
        )

    def own_copies(t):
        return (
            pltpu.make_async_copy(hsend.at[t, me], hrecv.at[t, OWN], own_sem.at[2 * t]),
            pltpu.make_async_copy(csend.at[t, me], crecv.at[t, OWN], own_sem.at[2 * t + 1]),
        )


    def lanes_of(u):
        return pl.ds(pl.multiple_of(128 * u, 128), 128)

    def build_head(u, _):
        t, tile = u // 4, u % 4
        lanes = lanes_of(u)
        j_tile = swap_blocks([jones[:, s, lanes] for s in range(4)])
        d_tile = swap_blocks([dual[:, s, lanes] for s in range(4)])
        for a in range(4):
            d = 4 * tile + a
            chan = 4 * u + a
            smooth = const[0] * basis_at(basis, 0, chan)
            for m in range(1, NTERMS):
                smooth = smooth + const[m] * basis_at(basis, m, chan)
            dual_t[chan] = d_tile[a]
            hsend[t, d, 0:8, :] = j_tile[a]
            hsend[t, d, 16:24, :] = PENALTY * smooth - d_tile[a]
        return 0

    def build_c(u, _):
        t, tile = u // 4, u % 4
        lanes = lanes_of(u)
        rows = jnp.concatenate(
            [coh[:, BAND * q : BAND * q + BAND, lanes].reshape(8 * BAND, 128) for q in range(QUARTERS)],
            axis=1,
        )
        out = dot(rows, perm[...])
        for a in range(4):
            csend[t, 4 * tile + a] = out[:, 128 * a : 128 * a + 128].reshape(8, BAND, 128)
        return 0

    at_row = lax.broadcasted_iota(jnp.int32, (128, 128), 0)
    apart = at_row - lax.broadcasted_iota(jnp.int32, (128, 128), 1)
    for a in range(4):
        for q in range(QUARTERS):
            hit = (apart == DIRS * (a - q)) & (lax.shift_right_logical(at_row, 5) == a)
            perm[128 * q : 128 * q + 128, 128 * a : 128 * a + 128] = jnp.where(hit, 1.0, 0.0).astype(BF16)

    for load in loads[:6]:
        load.wait()
    for m in range(NTERMS):
        for s in range(4):
            const[m, :, DIRS * s : DIRS * s + DIRS] = cons[m, :, s, :]
    meta[...] = jnp.zeros_like(meta)
    meta[0:2, 0:64] = pairs[...].astype(F32)
    meta[2:3, 0:64] = span[...].astype(F32)
    def build_heads(t):
        for i in range(4):
            pair = [vis[2 * i + half, PEERS * t : PEERS * t + PEERS, :] for half in range(2)]
            hsend[t, :, 8 + i, :] = jnp.concatenate(pair, axis=1)
        for d in range(PEERS):
            hsend[t, d, 12:16, :] = meta[0:4, :]
        lax.fori_loop(4 * t, 4 * t + 4, build_head, 0)

    build_heads(0)
    pl.semaphore_wait(barrier, PEERS - 1 + FREQS - 1)
    for t in range(STAGES):
        if t > 0:
            build_heads(t)
        own_copies(t)[0].start()
        each_peer(lambda group, i, t=t: h_copy(t, group, i).start())
        if t == 0:
            for load in loads[6:]:
                load.wait()
        lax.fori_loop(4 * t, 4 * t + 4, build_c, 0)
        own_copies(t)[1].start()
        each_peer(lambda group, i, t=t: c_copy(t, group, i).start())
        each_peer(lambda group, i, t=t: q_copy(t, group, i).start())

    row_block = lax.shift_right_logical(lax.broadcasted_iota(jnp.int32, (256, 128), 0), 5) & 3
    ones_blk[...] = jnp.where(row_block == lane_block((256, 128)), 1.0, 0.0).astype(BF16)

    band_mask = (lax.broadcasted_iota(jnp.int32, (BAND, 128), 1) & (BAND - 1)) == (
        lax.broadcasted_iota(jnp.int32, (BAND, 128), 0)
    )

    def banded(t, row):
        return jnp.concatenate(
            [
                jnp.where(band_mask, jnp.broadcast_to(hrecv[t, j, row : row + 1, :], (BAND, 128)), 0.0)
                for j in range(PEERS)
            ],
            axis=0,
        )

    def build_onehots():
        source = lax.broadcasted_iota(jnp.int32, (128, 256), 0)
        target = lax.broadcasted_iota(jnp.int32, (128, 256), 1)
        expand = jnp.where(
            lax.shift_right_logical(source, 4) == lax.shift_right_logical(target, 6), 1.0, 0.0
        ).astype(BF16)
        position = lax.broadcasted_iota(jnp.int32, (1, 256), 1) & (SLOTS - 1)
        j = position & (PEERS - 1)
        dz, dy = offset(0, j & 3)
        for group in range(1, 4):
            group_z, group_y = offset(group, j & 3)
            inside = lax.shift_right_logical(j, 2) == group
            dz = jnp.where(inside, group_z, dz)
            dy = jnp.where(inside, group_y, dy)
        owner_z = (z + RING - dz) & (RING - 1)
        owner_y = (y + RING - dy) & (RING - 1)
        label = 4 * (owner_z * RING + owner_y) + lax.shift_right_logical(position, 4)
        label = label.astype(F32)
        weight = dot(banded(0, 14).astype(BF16), expand)
        for side in range(2):
            station = dot(banded(0, 12 + side).astype(BF16), expand)
            hit = station == label
            onehot = jnp.where(hit, 1.0, 0.0).astype(BF16)
            ohg[ROWS * side : ROWS * side + ROWS, 0:256] = onehot
            ohg[ROWS * side : ROWS * side + ROWS, 256:512] = onehot
            weighted = jnp.transpose(jnp.where(hit, weight, 0.0)).astype(BF16)
            ohs[:, 512 * side : 512 * side + 256] = weighted
            ohs[:, 512 * side + 256 : 512 * side + 512] = weighted

    def build_visibility(t):
        source = lax.broadcasted_iota(jnp.int32, (256, 256), 0) & 127
        target = lax.broadcasted_iota(jnp.int32, (256, 256), 1)
        expand = jnp.where(
            lax.shift_right_logical(source, 4) == lax.shift_right_logical(target, 5), 1.0, 0.0
        ).astype(BF16)
        for i in range(4):
            high, low = halves(banded(t, 8 + i))
            out = dot(jnp.concatenate([high, low], axis=1), expand)
            vis_x[2 * i] = out[:, 0:128]
            vis_x[2 * i + 1] = out[:, 128:256]

    def unpack(t, first, target):
        block = lane_block((PEERS, 128))
        for c in range(8):
            flat = jnp.concatenate(
                [hrecv[t, j, first + c : first + c + 1, :] for j in range(PEERS)], axis=0
            )
            for s in range(4):
                target[c, PEERS * s : PEERS * s + PEERS] = spread_lanes(
                    jnp.where(block == s, flat, 0.0)
                )

    def gather():
        block = lane_block((SLOTS, 128))
        for c in range(8):
            for at, part in enumerate(halves(field[c])):
                for q in range(QUARTERS):
                    first = 256 * at + SLOTS * q
                    jrhs[first : first + SLOTS, 128 * c : 128 * c + 128] = jnp.where(
                        block == q, part.astype(F32), 0.0
                    ).astype(BF16)
        for c in range(4):
            jpq[:, 256 * c : 256 * c + 256] = dot(ohg[...], jrhs[:, 256 * c : 256 * c + 256])

    def process(t, group):
        size = GROUP * BAND
        first = pl.multiple_of(group * size, size)
        rows = pl.ds(first, size)
        sources = pl.ds(group * GROUP, GROUP)
        coherent = [crecv[t, sources, c].reshape(size, 128) for c in range(8)]
        left = [jpq[rows, 128 * c : 128 * c + 128] for c in range(8)]
        right = [jpq[pl.ds(ROWS + first, size), 128 * c : 128 * c + 128] for c in range(8)]
        applied = product_adjoint(coherent, right)
        model = product(left, applied)
        outer = product(left, coherent)
        split = [jnp.concatenate(halves(x), axis=1) for x in model]
        total = dot(jnp.concatenate(split, axis=0), ones_blk[...])
        misfit = [vis_x[c, rows, :] - total[size * c : size * c + size] for c in range(8)]
        for side in range(2):
            if side == 0:
                out = product_adjoint(misfit, applied) + square_right(applied)
            else:
                out = adjoint_product(misfit, outer) + square_left(outer)
            for c in range(12):
                for at, part in enumerate(halves(out[c])):
                    terms[pl.ds(ROWS * (2 * side + at) + first, size), 128 * c : 128 * c + 128] = part

    def solve():
        block = lane_block((SLOTS, 128))
        sums = []
        for pair in range(6):
            res = dot(ohs[...], terms[:, 256 * pair : 256 * pair + 256])
            for half in range(2):
                part = res[:, 128 * half : 128 * half + 128]
                total = jnp.where(block == 0, part[0:SLOTS], 0.0)
                for q in range(1, QUARTERS):
                    total = jnp.where(block == q, part[SLOTS * q : SLOTS * q + SLOTS], total)
                sums.append(spread_lanes(total))
        current = [field[c] for c in range(8)]
        rhs = [sums[c] + prior[c] - PENALTY * current[c] for c in range(8)]
        top = sums[8] + PENALTY
        bottom = sums[9] + PENALTY
        real, imag = sums[10], sums[11]
        scale = DAMPING / (top * bottom - real * real - imag * imag)
        for i in range(2):
            a, b = rhs[2 * i], rhs[2 * i + 1]
            c, d = rhs[4 + 2 * i], rhs[4 + 2 * i + 1]
            field[2 * i] = current[2 * i] + scale * (a * bottom - b * real - d * imag)
            field[2 * i + 1] = current[2 * i + 1] + scale * (b * top - a * real + c * imag)
            field[4 + 2 * i] = current[4 + 2 * i] + scale * (c * bottom - d * real + b * imag)
            field[5 + 2 * i] = current[5 + 2 * i] + scale * (d * top - c * real - a * imag)

    def send_back(t):
        block = lane_block((PEERS, 128))
        for c in range(8):
            whole = field[c]
            flat = jnp.where(block == 0, whole[0:PEERS], 0.0)
            for s in range(1, 4):
                flat = jnp.where(block == s, whole[PEERS * s : PEERS * s + PEERS], flat)
            for j in range(PEERS):
                rsend[t, j, c : c + 1, :] = flat[j : j + 1]
        rrecv[t, me] = rsend[t, OWN]
        each_peer(lambda group, i: r_copy(t, group, i).start())

    def stage(t, _):
        own = own_copies(t)
        own[0].wait()
        each_peer(lambda group, i: h_copy(t, group, i).wait_recv())

        @pl.when(t == 0)
        def _():
            build_onehots()

        build_visibility(t)
        unpack(t, 0, field)
        own[1].wait()

        def sweep(i, _):
            gather()

            def one_group(group, _):
                for source in range(4):
                    @pl.when((i == 0) & (group * 4 + source != OWN))
                    def _():
                        arrived(t, group * 4 + source).wait_recv()

                process(t, group)
                return 0

            lax.fori_loop(0, PEERS // GROUP, one_group, 0)
            @pl.when(i == 0)
            def _():
                each_peer(lambda group, i: q_copy(t, group, i).wait_recv())
                unpack(t, HEAD, prior)

            solve()
            return 0

        lax.fori_loop(0, ITERS, sweep, 0)
        send_back(t)
        return 0

    lax.fori_loop(0, STAGES, stage, 0)

    def project(t, projected):
        each_peer(lambda group, i: r_copy(t, group, i).wait_recv())

        def one(d, projected):
            chan = PEERS * t + d
            blended = rrecv[t, d] + dual_t[chan] * (1.0 / PENALTY)
            return tuple(
                projected[m] + blended * (basis_at(basis, m, chan) * (1.0 / norm_of(m)))
                for m in range(NTERMS)
            )

        return lax.fori_loop(0, PEERS, one, projected)

    lane = lane_block((1, 128))

    def basis_rows(u, _):
        for m in range(NTERMS):
            row = jnp.full((1, 128), basis_at(basis, m, 4 * u), F32)
            for a in range(1, 4):
                row = jnp.where(lane == a, basis_at(basis, m, 4 * u + a), row)
            rows_out[m : m + 1, lanes_of(u)] = PENALTY * row
        return 0

    def finish(u, _):
        lanes = lanes_of(u)
        t, tile = u // 4, u % 4
        parts = swap_blocks([rrecv[t, 4 * tile + a] for a in range(4)])
        for s in range(4):
            jones_out[:, s, lanes] = parts[s]
            lifted_out[:, s, lanes] = dual[:, s, lanes] + PENALTY * parts[s]
        return 0

    def sent(t, _):
        for copy in (h_copy, q_copy, c_copy):
            each_peer(lambda group, i, copy=copy: copy(t, group, i).wait_send())
        return 0

    projected = project(0, tuple(jnp.zeros((8, 128), F32) for _ in range(NTERMS)))
    lax.fori_loop(0, 8, basis_rows, 0)
    lax.fori_loop(0, 4, finish, 0)
    lax.fori_loop(0, STAGES, sent, 0)
    projected = project(1, projected)
    for m in range(NTERMS):
        psend[m] = projected[m]
        precv[fr, m] = projected[m]
    for g in (4, 5, 3, 6, 2, 7, 1):
        p_copy(g).start()
    lax.fori_loop(4, 8, finish, 0)
    for t in range(STAGES):
        each_peer(lambda group, i, t=t: r_copy(t, group, i).wait_send())
    for g in range(1, FREQS):
        p_copy(g).wait()
    block = lane_block((8, 128))
    for m in range(NTERMS):
        total = precv[0, m]
        for g in range(1, FREQS):
            total = total + precv[g, m]
        for s in range(4):
            smooth_out[m, :, s, :] = spread_lanes(jnp.where(block == s, total, 0.0))


def finish_kernel(jones, lifted, smooth, rows, jones_out, dual_hbm, cons_hbm, dual_out, cons_out, sem):
    copy = pltpu.make_async_copy(jones, jones_out, sem.at[0])
    copy.start()
    for m in range(NTERMS):
        cons_out[m] = smooth[m, :, :, 0:DIRS]
    cons_copy = pltpu.make_async_copy(cons_out, cons_hbm, sem.at[1])
    cons_copy.start()
    for tile in range(8):
        lanes = slice(128 * tile, 128 * tile + 128)
        scale = [jnp.broadcast_to(rows[m : m + 1, lanes], (4, 128)) for m in range(NTERMS)]
        for c in range(8):
            fitted = scale[0] * smooth[0, c]
            for m in range(1, NTERMS):
                fitted = fitted + scale[m] * smooth[m, c]
            dual_out[c, :, lanes] = lifted[c, :, lanes] - fitted
    dual_copy = pltpu.make_async_copy(dual_out, dual_hbm, sem.at[2])
    dual_copy.start()
    copy.wait()
    cons_copy.wait()
    dual_copy.wait()


def shards(coherency, visibility, span_lengths, station_pairs, jones_field, dual_field, consensus):
    vmem = pl.BlockSpec(memory_space=pltpu.VMEM)
    smem = pl.BlockSpec(memory_space=pltpu.SMEM)
    hbm = pl.BlockSpec(memory_space=pltpu.HBM)
    dma = pltpu.SemaphoreType.DMA
    basis = jnp.asarray(basis_table())
    operands = (
        coherency,
        jnp.transpose(visibility, (0, 2, 1)),
        span_lengths.reshape(1, -1),
        station_pairs,
        jones_field,
        dual_field,
        consensus,
    )
    jones, lifted, smooth, rows = pl.pallas_call(
        kernel,
        out_shape=(
            jax.ShapeDtypeStruct(jones_field.shape, F32),
            jax.ShapeDtypeStruct(dual_field.shape, F32),
            jax.ShapeDtypeStruct((NTERMS, 8, 4, 128), F32),
            jax.ShapeDtypeStruct((NTERMS, jones_field.shape[2]), F32),
        ),
        in_specs=[smem] + [hbm] * 7,
        out_specs=(vmem,) * 4,
        scratch_shapes=[pltpu.VMEM(x.shape, x.dtype) for x in operands]
        + [
            pltpu.VMEM((512, 512), BF16),
            pltpu.VMEM((STAGES, PEERS, 8, BAND, 128), F32),
            pltpu.VMEM((STAGES, PEERS, 8, BAND, 128), F32),
            pltpu.VMEM((STAGES, PEERS, HEAD + 8, 128), F32),
            pltpu.VMEM((STAGES, PEERS, HEAD + 8, 128), F32),
            pltpu.VMEM((STAGES, PEERS, 8, 128), F32),
            pltpu.VMEM((STAGES, PEERS, 8, 128), F32),
            pltpu.VMEM((NTERMS, 8, 128), F32),
            pltpu.VMEM((FREQS, NTERMS, 8, 128), F32),
            pltpu.VMEM((8, 128), F32),
            pltpu.VMEM((NTERMS, 8, 128), F32),
            pltpu.VMEM((STAGES * PEERS, 8, 128), F32),
            pltpu.VMEM((2 * ROWS, 8 * 128), F32),
            pltpu.VMEM((8, ROWS, 128), F32),
            pltpu.VMEM((4 * ROWS, 12 * 128), BF16),
            pltpu.VMEM((2 * ROWS, 512), BF16),
            pltpu.VMEM((QUARTERS * SLOTS, 4 * ROWS), BF16),
            pltpu.VMEM((2 * QUARTERS * SLOTS, 8 * 128), BF16),
            pltpu.VMEM((256, 128), BF16),
            pltpu.VMEM((8, SLOTS, 128), F32),
            pltpu.VMEM((8, SLOTS, 128), F32),
            dma((STAGES, PEERS)),
            dma((STAGES, PEERS)),
            dma((STAGES, PEERS)),
            dma((STAGES, PEERS)),
            dma((STAGES, PEERS)),
            dma((STAGES, PEERS)),
            dma((FREQS,)),
            dma((FREQS,)),
            dma((2 * STAGES,)),
            dma((7,)),
            dma((STAGES, PEERS)),
            dma((STAGES, PEERS)),
        ],
        compiler_params=pltpu.CompilerParams(
            collective_id=0, has_side_effects=True, vmem_limit_bytes=60 * 2**20
        ),
        name="calibrate",
    )(basis, *operands)
    return pl.pallas_call(
        finish_kernel,
        out_shape=(
            jax.ShapeDtypeStruct(jones_field.shape, F32),
            jax.ShapeDtypeStruct(dual_field.shape, F32),
            jax.ShapeDtypeStruct(consensus.shape, F32),
        ),
        in_specs=[vmem] * 4,
        out_specs=(hbm, hbm, hbm),
        scratch_shapes=[pltpu.VMEM(dual_field.shape, F32), pltpu.VMEM(consensus.shape, F32), dma((3,))],
        name="finish",
    )(jones, lifted, smooth, rows)


def solution(mesh):
    in_specs = (
        P(None, "bl", "freq"),
        P(None, "bl", "freq"),
        P("bl"),
        P(None, "bl"),
        P(None, "bl", "freq"),
        P(None, "bl", "freq"),
        P(None, None, "bl", None),
    )
    out_specs = (P(None, "bl", "freq"), P(None, "bl", "freq"), P(None, None, "bl", None))
    return jax.shard_map(shards, mesh=mesh, in_specs=in_specs, out_specs=out_specs, check_vma=False)
```

```python
import functools

import jax
import jax.numpy as jnp
import numpy as np
from jax import lax
from jax.experimental import pallas as pl
from jax.experimental.pallas import tpu as pltpu
from jax.sharding import PartitionSpec as P

CHANS = 256
ITERS = 2
NTERMS = 4
PENALTY = 4.0
DAMPING = 0.5

RING = 4
PEERS = 16
FREQS = 8
STAGES = 2
QUARTERS = 4
BAND = 16
DIRS = 32
SLOTS = 64
ROWS = PEERS * BAND
HEAD = 16
GROUP = 4
OWN = 4

MESH = pl.DeviceIdType.MESH
F32 = jnp.float32
BF16 = jnp.bfloat16


def basis_table():
    channel = np.arange(CHANS, dtype=np.float64) + 0.5
    order = np.arange(NTERMS, dtype=np.float64)
    return np.cos(np.pi * order[:, None] * channel[None, :] / CHANS).astype(np.float32)


def norm_of(term):
    return float(CHANS) if term == 0 else 0.5 * CHANS


def product(a, b):
    real, imag = [], []
    for i in range(2):
        for j in range(2):
            real.append(
                a[2 * i] * b[j]
                + a[2 * i + 1] * b[2 + j]
                - a[4 + 2 * i] * b[4 + j]
                - a[4 + 2 * i + 1] * b[4 + 2 + j]
            )
            imag.append(
                a[2 * i] * b[4 + j]
                + a[2 * i + 1] * b[4 + 2 + j]
                + a[4 + 2 * i] * b[j]
                + a[4 + 2 * i + 1] * b[2 + j]
            )
    return real + imag


def product_adjoint(a, b):
    real, imag = [], []
    for i in range(2):
        for j in range(2):
            real.append(
                a[2 * i] * b[2 * j]
                + a[2 * i + 1] * b[2 * j + 1]
                + a[4 + 2 * i] * b[4 + 2 * j]
                + a[4 + 2 * i + 1] * b[4 + 2 * j + 1]
            )
            imag.append(
                a[4 + 2 * i] * b[2 * j]
                + a[4 + 2 * i + 1] * b[2 * j + 1]
                - a[2 * i] * b[4 + 2 * j]
                - a[2 * i + 1] * b[4 + 2 * j + 1]
            )
    return real + imag


def adjoint_product(a, b):
    real, imag = [], []
    for i in range(2):
        for j in range(2):
            real.append(
                a[i] * b[j] + a[2 + i] * b[2 + j] + a[4 + i] * b[4 + j] + a[6 + i] * b[6 + j]
            )
            imag.append(
                a[i] * b[4 + j] + a[2 + i] * b[6 + j] - a[4 + i] * b[j] - a[6 + i] * b[2 + j]
            )
    return real + imag


def square_right(a):
    top = a[0] * a[0] + a[1] * a[1] + a[4] * a[4] + a[5] * a[5]
    bottom = a[2] * a[2] + a[3] * a[3] + a[6] * a[6] + a[7] * a[7]
    real = a[0] * a[2] + a[4] * a[6] + a[1] * a[3] + a[5] * a[7]
    imag = a[4] * a[2] - a[0] * a[6] + a[5] * a[3] - a[1] * a[7]
    return [top, bottom, real, imag]


def square_left(a):
    return square_right([a[0], a[2], a[1], a[3], -a[4], -a[6], -a[5], -a[7]])


def halves(x):
    high = x.astype(BF16)
    return high, (x - high.astype(F32)).astype(BF16)


def lane_block(shape):
    return lax.shift_right_logical(lax.broadcasted_iota(jnp.int32, shape, len(shape) - 1), 5)


def swap_blocks(x):
    block = lane_block(x[0].shape)
    left = block < 2
    even = (block & 1) == 0
    halfway = [None] * 4
    for low in range(2):
        first, second = x[low], x[2 + low]
        halfway[low] = jnp.where(left, first, pltpu.roll(second, 64, 1))
        halfway[2 + low] = jnp.where(left, pltpu.roll(first, 64, 1), second)
    out = [None] * 4
    for high in range(2):
        first, second = halfway[2 * high], halfway[2 * high + 1]
        out[2 * high] = jnp.where(even, first, pltpu.roll(second, 32, 1))
        out[2 * high + 1] = jnp.where(even, pltpu.roll(first, 96, 1), second)
    return out


def spread_lanes(x):
    x = x + pltpu.roll(x, 64, 1)
    return x + pltpu.roll(x, 32, 1)


def dot(a, b):
    return jnp.dot(a, b, preferred_element_type=F32)


def basis_at(basis, term, chan):
    return basis[term, lax.axis_index("freq") * (CHANS // FREQS) + chan]


def offset(group, i):
    low, high = i % 2, i // 2
    sign = 1 + 2 * high
    if group == 0:
        return 2 * (1 - low) + sign * low, sign * (1 - low) + 2 * low
    if group == 1:
        return 2 * low, 2 * ((low + high) % 2)
    if group == 2:
        return 1 + 2 * low, 1 + 2 * ((low + high) % 2)
    return low * sign, (1 - low) * sign


def kernel(
    basis, coh_hbm, vis_hbm, span_hbm, pairs_hbm, jones_hbm, dual_hbm, cons_hbm,
    jones_out, lifted_out, smooth_out, rows_out,
    coh, vis, span, pairs, jones, dual, cons,
    perm, csend, crecv, hsend, hrecv, rsend, rrecv, psend, precv,
    meta, const, dual_t, jpq, vis_x, terms, ohg, ohs, jrhs, ones_blk, field, prior,
    csend_sem, crecv_sem, hsend_sem, hrecv_sem, rsend_sem, rrecv_sem, psend_sem, precv_sem, own_sem, in_sem, qsend_sem, qrecv_sem,
):
    me = lax.axis_index("bl")
    fr = lax.axis_index("freq")
    z, y = me // RING, me % RING

    def ahead(group, i):
        dz, dy = offset(group, i)
        return lax.rem(z + dz, RING) * RING + lax.rem(y + dy, RING)

    def behind(group, i):
        dz, dy = offset(group, i)
        return lax.rem(z + RING - dz, RING) * RING + lax.rem(y + RING - dy, RING)

    def each_peer(step, unroll=False):
        for group in range(4):
            def one(i, _, group=group):
                step(group, i)
                return 0

            first = 1 if group == OWN // GROUP else 0
            if unroll:
                for i in range(first, 4):
                    step(group, i)
            else:
                lax.fori_loop(first, 4, one, 0)

    def freq_ahead(g):
        return lax.rem(fr + g, FREQS)


    loads = [
        pltpu.make_async_copy(source, target, in_sem.at[i])
        for i, (source, target) in enumerate(
            [
                (jones_hbm, jones), (dual_hbm, dual), (cons_hbm, cons), (vis_hbm, vis),
                (span_hbm, span), (pairs_hbm, pairs), (coh_hbm, coh),
            ]
        )
    ]
    for load in loads:
        load.start()

    barrier = pltpu.get_barrier_semaphore()
    each_peer(
        lambda group, i: pl.semaphore_signal(
            barrier, inc=1, device_id={"bl": ahead(group, i)}, device_id_type=MESH
        ),
        unroll=True,
    )
    for g in range(1, FREQS):
        pl.semaphore_signal(barrier, inc=1, device_id={"freq": freq_ahead(g)}, device_id_type=MESH)

    def c_copy(t, group, i):
        j = 4 * group + i
        return pltpu.make_async_remote_copy(
            src_ref=csend.at[t, ahead(group, i)], dst_ref=crecv.at[t, j],
            send_sem=csend_sem.at[t, j], recv_sem=crecv_sem.at[t, j],
            device_id={"bl": ahead(group, i)}, device_id_type=MESH,
        )

    def h_copy(t, group, i):
        j = 4 * group + i
        return pltpu.make_async_remote_copy(
            src_ref=hsend.at[t, ahead(group, i), pl.ds(0, HEAD)], dst_ref=hrecv.at[t, j, pl.ds(0, HEAD)],
            send_sem=hsend_sem.at[t, j], recv_sem=hrecv_sem.at[t, j],
            device_id={"bl": ahead(group, i)}, device_id_type=MESH,
        )

    def q_copy(t, group, i):
        j = 4 * group + i
        return pltpu.make_async_remote_copy(
            src_ref=hsend.at[t, ahead(group, i), pl.ds(HEAD, 8)], dst_ref=hrecv.at[t, j, pl.ds(HEAD, 8)],
            send_sem=qsend_sem.at[t, j], recv_sem=qrecv_sem.at[t, j],
            device_id={"bl": ahead(group, i)}, device_id_type=MESH,
        )

    def r_copy(t, group, i):
        j = 4 * group + i
        return pltpu.make_async_remote_copy(
            src_ref=rsend.at[t, j], dst_ref=rrecv.at[t, me],
            send_sem=rsend_sem.at[t, j], recv_sem=rrecv_sem.at[t, j],
            device_id={"bl": behind(group, i)}, device_id_type=MESH,
        )

    def arrived(t, j):
        return pltpu.make_async_remote_copy(
            src_ref=csend.at[t, j], dst_ref=crecv.at[t, j],
            send_sem=csend_sem.at[t, j], recv_sem=crecv_sem.at[t, j],
            device_id={"bl": ahead(3, 0)}, device_id_type=MESH,
        )

    def p_copy(g):
        return pltpu.make_async_remote_copy(
            src_ref=psend, dst_ref=precv.at[fr],
            send_sem=psend_sem.at[g], recv_sem=precv_sem.at[g],
            device_id={"freq": freq_ahead(g)}, device_id_type=MESH,
        )

    def own_copies(t):
        return (
            pltpu.make_async_copy(hsend.at[t, me], hrecv.at[t, OWN], own_sem.at[2 * t]),
            pltpu.make_async_copy(csend.at[t, me], crecv.at[t, OWN], own_sem.at[2 * t + 1]),
        )


    def lanes_of(u):
        return pl.ds(pl.multiple_of(128 * u, 128), 128)

    def build_head(u, _):
        t, tile = u // 4, u % 4
        lanes = lanes_of(u)
        j_tile = swap_blocks([jones[:, s, lanes] for s in range(4)])
        d_tile = swap_blocks([dual[:, s, lanes] for s in range(4)])
        for a in range(4):
            d = 4 * tile + a
            chan = 4 * u + a
            smooth = const[0] * basis_at(basis, 0, chan)
            for m in range(1, NTERMS):
                smooth = smooth + const[m] * basis_at(basis, m, chan)
            dual_t[chan] = d_tile[a]
            hsend[t, d, 0:8, :] = j_tile[a]
            hsend[t, d, 16:24, :] = PENALTY * smooth - d_tile[a]
        return 0

    def build_c(u, _):
        t, tile = u // 4, u % 4
        lanes = lanes_of(u)
        rows = jnp.concatenate(
            [coh[:, BAND * q : BAND * q + BAND, lanes].reshape(8 * BAND, 128) for q in range(QUARTERS)],
            axis=1,
        )
        out = dot(rows, perm[...])
        for a in range(4):
            csend[t, 4 * tile + a] = out[:, 128 * a : 128 * a + 128].reshape(8, BAND, 128)
        return 0

    at_row = lax.broadcasted_iota(jnp.int32, (128, 128), 0)
    apart = at_row - lax.broadcasted_iota(jnp.int32, (128, 128), 1)
    for a in range(4):
        for q in range(QUARTERS):
            hit = (apart == DIRS * (a - q)) & (lax.shift_right_logical(at_row, 5) == a)
            perm[128 * q : 128 * q + 128, 128 * a : 128 * a + 128] = jnp.where(hit, 1.0, 0.0).astype(BF16)

    for load in loads[:6]:
        load.wait()
    for m in range(NTERMS):
        for s in range(4):
            const[m, :, DIRS * s : DIRS * s + DIRS] = cons[m, :, s, :]
    meta[...] = jnp.zeros_like(meta)
    meta[0:2, 0:64] = pairs[...].astype(F32)
    meta[2:3, 0:64] = span[...].astype(F32)
    def build_heads(t):
        for i in range(4):
            pair = [vis[2 * i + half, PEERS * t : PEERS * t + PEERS, :] for half in range(2)]
            hsend[t, :, 8 + i, :] = jnp.concatenate(pair, axis=1)
        for d in range(PEERS):
            hsend[t, d, 12:16, :] = meta[0:4, :]
        lax.fori_loop(4 * t, 4 * t + 4, build_head, 0)

    build_heads(0)
    pl.semaphore_wait(barrier, PEERS - 1 + FREQS - 1)
    for t in range(STAGES):
        if t > 0:
            build_heads(t)
        own_copies(t)[0].start()
        each_peer(lambda group, i, t=t: h_copy(t, group, i).start(), unroll=True)
        if t == 0:
            for load in loads[6:]:
                load.wait()
        lax.fori_loop(4 * t, 4 * t + 4, build_c, 0)
        own_copies(t)[1].start()
        each_peer(lambda group, i, t=t: c_copy(t, group, i).start(), unroll=True)
        each_peer(lambda group, i, t=t: q_copy(t, group, i).start())

    row_block = lax.shift_right_logical(lax.broadcasted_iota(jnp.int32, (256, 128), 0), 5) & 3
    ones_blk[...] = jnp.where(row_block == lane_block((256, 128)), 1.0, 0.0).astype(BF16)

    band_mask = (lax.broadcasted_iota(jnp.int32, (BAND, 128), 1) & (BAND - 1)) == (
        lax.broadcasted_iota(jnp.int32, (BAND, 128), 0)
    )

    def banded(t, row):
        return jnp.concatenate(
            [
                jnp.where(band_mask, jnp.broadcast_to(hrecv[t, j, row : row + 1, :], (BAND, 128)), 0.0)
                for j in range(PEERS)
            ],
            axis=0,
        )

    def build_onehots():
        source = lax.broadcasted_iota(jnp.int32, (128, 256), 0)
        target = lax.broadcasted_iota(jnp.int32, (128, 256), 1)
        expand = jnp.where(
            lax.shift_right_logical(source, 4) == lax.shift_right_logical(target, 6), 1.0, 0.0
        ).astype(BF16)
        position = lax.broadcasted_iota(jnp.int32, (1, 256), 1) & (SLOTS - 1)
        j = position & (PEERS - 1)
        dz, dy = offset(0, j & 3)
        for group in range(1, 4):
            group_z, group_y = offset(group, j & 3)
            inside = lax.shift_right_logical(j, 2) == group
            dz = jnp.where(inside, group_z, dz)
            dy = jnp.where(inside, group_y, dy)
        owner_z = (z + RING - dz) & (RING - 1)
        owner_y = (y + RING - dy) & (RING - 1)
        label = 4 * (owner_z * RING + owner_y) + lax.shift_right_logical(position, 4)
        label = label.astype(F32)
        weight = dot(banded(0, 14).astype(BF16), expand)
        for side in range(2):
            station = dot(banded(0, 12 + side).astype(BF16), expand)
            hit = station == label
            onehot = jnp.where(hit, 1.0, 0.0).astype(BF16)
            ohg[ROWS * side : ROWS * side + ROWS, 0:256] = onehot
            ohg[ROWS * side : ROWS * side + ROWS, 256:512] = onehot
            weighted = jnp.transpose(jnp.where(hit, weight, 0.0)).astype(BF16)
            ohs[:, 512 * side : 512 * side + 256] = weighted
            ohs[:, 512 * side + 256 : 512 * side + 512] = weighted

    def build_visibility(t):
        source = lax.broadcasted_iota(jnp.int32, (256, 256), 0) & 127
        target = lax.broadcasted_iota(jnp.int32, (256, 256), 1)
        expand = jnp.where(
            lax.shift_right_logical(source, 4) == lax.shift_right_logical(target, 5), 1.0, 0.0
        ).astype(BF16)
        for i in range(4):
            high, low = halves(banded(t, 8 + i))
            out = dot(jnp.concatenate([high, low], axis=1), expand)
            vis_x[2 * i] = out[:, 0:128]
            vis_x[2 * i + 1] = out[:, 128:256]

    def unpack(t, first, target):
        block = lane_block((PEERS, 128))
        for c in range(8):
            flat = jnp.concatenate(
                [hrecv[t, j, first + c : first + c + 1, :] for j in range(PEERS)], axis=0
            )
            for s in range(4):
                target[c, PEERS * s : PEERS * s + PEERS] = spread_lanes(
                    jnp.where(block == s, flat, 0.0)
                )

    def gather():
        block = lane_block((SLOTS, 128))
        for c in range(8):
            for at, part in enumerate(halves(field[c])):
                for q in range(QUARTERS):
                    first = 256 * at + SLOTS * q
                    jrhs[first : first + SLOTS, 128 * c : 128 * c + 128] = jnp.where(
                        block == q, part.astype(F32), 0.0
                    ).astype(BF16)
        for c in range(4):
            jpq[:, 256 * c : 256 * c + 256] = dot(ohg[...], jrhs[:, 256 * c : 256 * c + 256])

    def process(t, group):
        size = GROUP * BAND
        first = pl.multiple_of(group * size, size)
        rows = pl.ds(first, size)
        sources = pl.ds(group * GROUP, GROUP)
        coherent = [crecv[t, sources, c].reshape(size, 128) for c in range(8)]
        left = [jpq[rows, 128 * c : 128 * c + 128] for c in range(8)]
        right = [jpq[pl.ds(ROWS + first, size), 128 * c : 128 * c + 128] for c in range(8)]
        applied = product_adjoint(coherent, right)
        model = product(left, applied)
        outer = product(left, coherent)
        split = [jnp.concatenate(halves(x), axis=1) for x in model]
        total = dot(jnp.concatenate(split, axis=0), ones_blk[...])
        misfit = [vis_x[c, rows, :] - total[size * c : size * c + size] for c in range(8)]
        for side in range(2):
            if side == 0:
                out = product_adjoint(misfit, applied) + square_right(applied)
            else:
                out = adjoint_product(misfit, outer) + square_left(outer)
            for c in range(12):
                for at, part in enumerate(halves(out[c])):
                    terms[pl.ds(ROWS * (2 * side + at) + first, size), 128 * c : 128 * c + 128] = part

    def solve():
        block = lane_block((SLOTS, 128))
        sums = []
        for pair in range(6):
            res = dot(ohs[...], terms[:, 256 * pair : 256 * pair + 256])
            for half in range(2):
                part = res[:, 128 * half : 128 * half + 128]
                total = jnp.where(block == 0, part[0:SLOTS], 0.0)
                for q in range(1, QUARTERS):
                    total = jnp.where(block == q, part[SLOTS * q : SLOTS * q + SLOTS], total)
                sums.append(spread_lanes(total))
        current = [field[c] for c in range(8)]
        rhs = [sums[c] + prior[c] - PENALTY * current[c] for c in range(8)]
        top = sums[8] + PENALTY
        bottom = sums[9] + PENALTY
        real, imag = sums[10], sums[11]
        scale = DAMPING / (top * bottom - real * real - imag * imag)
        for i in range(2):
            a, b = rhs[2 * i], rhs[2 * i + 1]
            c, d = rhs[4 + 2 * i], rhs[4 + 2 * i + 1]
            field[2 * i] = current[2 * i] + scale * (a * bottom - b * real - d * imag)
            field[2 * i + 1] = current[2 * i + 1] + scale * (b * top - a * real + c * imag)
            field[4 + 2 * i] = current[4 + 2 * i] + scale * (c * bottom - d * real + b * imag)
            field[5 + 2 * i] = current[5 + 2 * i] + scale * (d * top - c * real - a * imag)

    def send_back(t):
        block = lane_block((PEERS, 128))
        for c in range(8):
            whole = field[c]
            flat = jnp.where(block == 0, whole[0:PEERS], 0.0)
            for s in range(1, 4):
                flat = jnp.where(block == s, whole[PEERS * s : PEERS * s + PEERS], flat)
            for j in range(PEERS):
                rsend[t, j, c : c + 1, :] = flat[j : j + 1]
        rrecv[t, me] = rsend[t, OWN]
        each_peer(lambda group, i: r_copy(t, group, i).start(), unroll=True)

    def stage(t, _):
        own = own_copies(t)
        own[0].wait()
        each_peer(lambda group, i: h_copy(t, group, i).wait_recv())

        @pl.when(t == 0)
        def _():
            build_onehots()

        build_visibility(t)
        unpack(t, 0, field)
        own[1].wait()

        def sweep(i, _):
            gather()

            def one_group(group, _):
                for source in range(4):
                    @pl.when((i == 0) & (group * 4 + source != OWN))
                    def _():
                        arrived(t, group * 4 + source).wait_recv()

                process(t, group)
                return 0

            lax.fori_loop(0, PEERS // GROUP, one_group, 0)
            @pl.when(i == 0)
            def _():
                each_peer(lambda group, i: q_copy(t, group, i).wait_recv())
                unpack(t, HEAD, prior)

            solve()
            return 0

        lax.fori_loop(0, ITERS, sweep, 0)
        send_back(t)
        return 0

    lax.fori_loop(0, STAGES, stage, 0)

    def project(t, projected):
        each_peer(lambda group, i: r_copy(t, group, i).wait_recv())

        def one(d, projected):
            chan = PEERS * t + d
            blended = rrecv[t, d] + dual_t[chan] * (1.0 / PENALTY)
            return tuple(
                projected[m] + blended * (basis_at(basis, m, chan) * (1.0 / norm_of(m)))
                for m in range(NTERMS)
            )

        return lax.fori_loop(0, PEERS, one, projected)

    lane = lane_block((1, 128))

    def basis_rows(u, _):
        for m in range(NTERMS):
            row = jnp.full((1, 128), basis_at(basis, m, 4 * u), F32)
            for a in range(1, 4):
                row = jnp.where(lane == a, basis_at(basis, m, 4 * u + a), row)
            rows_out[m : m + 1, lanes_of(u)] = PENALTY * row
        return 0

    def finish(u, _):
        lanes = lanes_of(u)
        t, tile = u // 4, u % 4
        parts = swap_blocks([rrecv[t, 4 * tile + a] for a in range(4)])
        for s in range(4):
            jones_out[:, s, lanes] = parts[s]
            lifted_out[:, s, lanes] = dual[:, s, lanes] + PENALTY * parts[s]
        return 0

    def sent(t, _):
        for copy in (h_copy, q_copy, c_copy):
            each_peer(lambda group, i, copy=copy: copy(t, group, i).wait_send())
        return 0

    projected = project(0, tuple(jnp.zeros((8, 128), F32) for _ in range(NTERMS)))
    lax.fori_loop(0, 8, basis_rows, 0)
    lax.fori_loop(0, 4, finish, 0)
    lax.fori_loop(0, STAGES, sent, 0)
    projected = project(1, projected)
    for m in range(NTERMS):
        psend[m] = projected[m]
        precv[fr, m] = projected[m]
    for g in (4, 5, 3, 6, 2, 7, 1):
        p_copy(g).start()
    lax.fori_loop(4, 8, finish, 0)
    for t in range(STAGES):
        each_peer(lambda group, i, t=t: r_copy(t, group, i).wait_send())
    for g in range(1, FREQS):
        p_copy(g).wait()
    block = lane_block((8, 128))
    for m in range(NTERMS):
        total = precv[0, m]
        for g in range(1, FREQS):
            total = total + precv[g, m]
        for s in range(4):
            smooth_out[m, :, s, :] = spread_lanes(jnp.where(block == s, total, 0.0))


def finish_kernel(jones, lifted, smooth, rows, jones_out, dual_hbm, cons_hbm, dual_out, cons_out, sem):
    copy = pltpu.make_async_copy(jones, jones_out, sem.at[0])
    copy.start()
    for m in range(NTERMS):
        cons_out[m] = smooth[m, :, :, 0:DIRS]
    cons_copy = pltpu.make_async_copy(cons_out, cons_hbm, sem.at[1])
    cons_copy.start()
    for tile in range(8):
        lanes = slice(128 * tile, 128 * tile + 128)
        scale = [jnp.broadcast_to(rows[m : m + 1, lanes], (4, 128)) for m in range(NTERMS)]
        for c in range(8):
            fitted = scale[0] * smooth[0, c]
            for m in range(1, NTERMS):
                fitted = fitted + scale[m] * smooth[m, c]
            dual_out[c, :, lanes] = lifted[c, :, lanes] - fitted
    dual_copy = pltpu.make_async_copy(dual_out, dual_hbm, sem.at[2])
    dual_copy.start()
    copy.wait()
    cons_copy.wait()
    dual_copy.wait()


def shards(coherency, visibility, span_lengths, station_pairs, jones_field, dual_field, consensus):
    vmem = pl.BlockSpec(memory_space=pltpu.VMEM)
    smem = pl.BlockSpec(memory_space=pltpu.SMEM)
    hbm = pl.BlockSpec(memory_space=pltpu.HBM)
    dma = pltpu.SemaphoreType.DMA
    basis = jnp.asarray(basis_table())
    operands = (
        coherency,
        jnp.transpose(visibility, (0, 2, 1)),
        span_lengths.reshape(1, -1),
        station_pairs,
        jones_field,
        dual_field,
        consensus,
    )
    jones, lifted, smooth, rows = pl.pallas_call(
        kernel,
        out_shape=(
            jax.ShapeDtypeStruct(jones_field.shape, F32),
            jax.ShapeDtypeStruct(dual_field.shape, F32),
            jax.ShapeDtypeStruct((NTERMS, 8, 4, 128), F32),
            jax.ShapeDtypeStruct((NTERMS, jones_field.shape[2]), F32),
        ),
        in_specs=[smem] + [hbm] * 7,
        out_specs=(vmem,) * 4,
        scratch_shapes=[pltpu.VMEM(x.shape, x.dtype) for x in operands]
        + [
            pltpu.VMEM((512, 512), BF16),
            pltpu.VMEM((STAGES, PEERS, 8, BAND, 128), F32),
            pltpu.VMEM((STAGES, PEERS, 8, BAND, 128), F32),
            pltpu.VMEM((STAGES, PEERS, HEAD + 8, 128), F32),
            pltpu.VMEM((STAGES, PEERS, HEAD + 8, 128), F32),
            pltpu.VMEM((STAGES, PEERS, 8, 128), F32),
            pltpu.VMEM((STAGES, PEERS, 8, 128), F32),
            pltpu.VMEM((NTERMS, 8, 128), F32),
            pltpu.VMEM((FREQS, NTERMS, 8, 128), F32),
            pltpu.VMEM((8, 128), F32),
            pltpu.VMEM((NTERMS, 8, 128), F32),
            pltpu.VMEM((STAGES * PEERS, 8, 128), F32),
            pltpu.VMEM((2 * ROWS, 8 * 128), F32),
            pltpu.VMEM((8, ROWS, 128), F32),
            pltpu.VMEM((4 * ROWS, 12 * 128), BF16),
            pltpu.VMEM((2 * ROWS, 512), BF16),
            pltpu.VMEM((QUARTERS * SLOTS, 4 * ROWS), BF16),
            pltpu.VMEM((2 * QUARTERS * SLOTS, 8 * 128), BF16),
            pltpu.VMEM((256, 128), BF16),
            pltpu.VMEM((8, SLOTS, 128), F32),
            pltpu.VMEM((8, SLOTS, 128), F32),
            dma((STAGES, PEERS)),
            dma((STAGES, PEERS)),
            dma((STAGES, PEERS)),
            dma((STAGES, PEERS)),
            dma((STAGES, PEERS)),
            dma((STAGES, PEERS)),
            dma((FREQS,)),
            dma((FREQS,)),
            dma((2 * STAGES,)),
            dma((7,)),
            dma((STAGES, PEERS)),
            dma((STAGES, PEERS)),
        ],
        compiler_params=pltpu.CompilerParams(
            collective_id=0, has_side_effects=True, vmem_limit_bytes=60 * 2**20
        ),
        name="calibrate",
    )(basis, *operands)
    return pl.pallas_call(
        finish_kernel,
        out_shape=(
            jax.ShapeDtypeStruct(jones_field.shape, F32),
            jax.ShapeDtypeStruct(dual_field.shape, F32),
            jax.ShapeDtypeStruct(consensus.shape, F32),
        ),
        in_specs=[vmem] * 4,
        out_specs=(hbm, hbm, hbm),
        scratch_shapes=[pltpu.VMEM(dual_field.shape, F32), pltpu.VMEM(consensus.shape, F32), dma((3,))],
        name="finish",
    )(jones, lifted, smooth, rows)


def solution(mesh):
    in_specs = (
        P(None, "bl", "freq"),
        P(None, "bl", "freq"),
        P("bl"),
        P(None, "bl"),
        P(None, "bl", "freq"),
        P(None, "bl", "freq"),
        P(None, None, "bl", None),
    )
    out_specs = (P(None, "bl", "freq"), P(None, "bl", "freq"), P(None, None, "bl", None))
    return jax.shard_map(shards, mesh=mesh, in_specs=in_specs, out_specs=out_specs, check_vma=False)
```
